32 devices in a mesh: seg: 8 (over z, x), tp: 4 (over y, core).
Axes of the slice: x: 2, y: 2, z: 4, core: 2. Of those that a mesh axis runs over, the one named last changes fastest.
Arguments:
- queries: bfloat16 [2048, 8192], P('seg', 'tp'), may hold values from -8 to 8
- keys_own: bfloat16 [2048, 1024], P('seg', 'tp'), may hold values from -8 to 8
- values_own: bfloat16 [2048, 1024], P('seg', 'tp'), may hold values from -6 to 6
- out_grad: bfloat16 [2048, 8192], P('seg', 'tp'), may hold values from -6 to 6
- summary_states: bfloat16 [400, 8192], P('seg'), may hold values from -6 to 6
- w_key: bfloat16 [8192, 1024], P(None, 'tp'), may hold values from -0.0625 to 0.0625
- w_value: bfloat16 [8192, 1024], P(None, 'tp'), may hold values from -0.0625 to 0.0625
- summary_grad: bfloat16 [400, 8192], P('seg', 'tp'), may hold values from -6 to 6
Outputs:
- query_grad: bfloat16 [2048, 8192], P('seg', 'tp')
- key_grad: bfloat16 [2048, 1024], P('seg', 'tp')
- value_grad: bfloat16 [2048, 1024], P('seg', 'tp')
- state_grad: bfloat16 [400, 8192], P('seg', 'tp')
The draws below stay inside these ranges and needn't reach their ends.
All inputs are finite; a program needn't handle non-finite values.
Results may differ from the reference program's by a relative error of at most 0.023.
Values may be sent and summed in bfloat16 or wider, within the bound.
No kernel may reach another device: no remote copies, remote signals or barrier semaphores. Data moves between devices by JAX's collectives and lax.ppermute only.
A program may use at most 256 MiB of HBM per device.

```python
import jax
import jax.numpy as jnp
from jax import lax

D = 8192
HEADS = 64
KVH = 8
HD = 128
M = 50
TOK_DEV = 256
TOKENS = 2048
NSUM = 400
N_SEG = 8


def noise_field(key, width):
    return jnp.clip(jax.random.normal(key, (TOKENS, width), jnp.float32), -6.0, 6.0)


def draw_queries(key, part):
    base_noise = noise_field(jax.random.fold_in(key, 11), HEADS * HD)
    return base_noise.astype(jnp.bfloat16)


def draw_keys_own(key, part):
    base_noise = noise_field(jax.random.fold_in(key, 12), KVH * HD)
    return base_noise.astype(jnp.bfloat16)


def levels(key, shape, pieces, smallest, high):
    def one(axis_at, parts):
        heights = jax.random.uniform(jax.random.fold_in(jax.random.fold_in(key, 6), axis_at), (parts,), jnp.float32, smallest / len(pieces), high / len(pieces))
        return jnp.repeat(jnp.exp(heights), shape[axis_at] // parts).reshape((-1,) + (1,) * (len(shape) - axis_at - 1))

    level = one(*pieces[0])
    for cut in pieces[1:]:
        level = level * one(*cut)
    return level


def noise(own_key, shape, scale, most, split=(), dtype=jnp.bfloat16):
    level = levels(own_key, shape, split, -0.22, 0.18) if split else 1.0
    result = jax.random.normal(own_key, shape, jnp.float32) * scale * level
    return jnp.minimum(jnp.maximum(result, -most), most).astype(dtype)


def setup_inputs(seed: int = 0) -> dict:
    arg_keys = jax.random.split(jax.random.key(seed), 9)
    queries = draw_queries(jax.random.fold_in(arg_keys[8], 71), 0)
    keys_own = draw_keys_own(jax.random.fold_in(arg_keys[8], 71), 0)
    values_own = noise(arg_keys[2], (TOKENS, KVH * HD), 1.0, 6.0, ((0, 8), (1, 4)))
    out_grad = noise(arg_keys[3], (TOKENS, HEADS * HD), 1.0, 6.0, ((0, 8), (1, 4)))
    summary_states = noise(arg_keys[4], (NSUM, D), 1.0, 6.0, ((0, 8),))
    w_key = noise(arg_keys[5], (D, KVH * HD), D ** -0.5, 0.0625, ((1, 4),))
    w_value = noise(arg_keys[6], (D, KVH * HD), D ** -0.5, 0.0625, ((1, 4),))
    summary_grad = noise(arg_keys[7], (NSUM, D), 1.0, 6.0, ((0, 8), (1, 4)))
    return dict(queries=queries, keys_own=keys_own, values_own=values_own, out_grad=out_grad, summary_states=summary_states, w_key=w_key, w_value=w_value, summary_grad=summary_grad)


def reference(queries, keys_own, values_own, out_grad, summary_states, w_key, w_value, summary_grad):
    group = HEADS // KVH
    scale = HD ** -0.5
    nsum = M * N_SEG
    nkeys = nsum + TOK_DEV
    sum_keys = jnp.dot(summary_states, w_key, preferred_element_type=jnp.float32).astype(jnp.bfloat16)
    sum_vals = jnp.dot(summary_states, w_value, preferred_element_type=jnp.float32).astype(jnp.bfloat16)
    row_pos = jnp.arange(TOK_DEV)[:, None]
    col_pos = jnp.arange(nkeys)[None, :]
    acc_keys = jnp.zeros((nsum, KVH, HD), jnp.float32)
    acc_vals = jnp.zeros((nsum, KVH, HD), jnp.float32)
    query_parts = []
    key_parts = []
    value_parts = []
    for segment in range(N_SEG):
        lo = segment * TOK_DEV
        hi = lo + TOK_DEV
        keyset = jnp.concatenate([sum_keys, keys_own[lo:hi]], 0).reshape(nkeys, KVH, HD).astype(jnp.float32)
        valset = jnp.concatenate([sum_vals, values_own[lo:hi]], 0).reshape(nkeys, KVH, HD).astype(jnp.float32)
        query = queries[lo:hi].reshape(TOK_DEV, KVH, group, HD).astype(jnp.float32)
        grad = out_grad[lo:hi].reshape(TOK_DEV, KVH, group, HD).astype(jnp.float32)
        visible = jnp.where(col_pos < nsum, col_pos < segment * M, (col_pos - nsum) <= row_pos)
        scores = jnp.einsum('snhd,knd->nhsk', query, keyset) * scale
        scores = jnp.where(visible, scores, -jnp.inf)
        probs = jnp.exp(scores - jnp.max(scores, axis=-1, keepdims=True))
        probs = probs / jnp.sum(probs, axis=-1, keepdims=True)
        probs_b = probs.astype(jnp.bfloat16).astype(jnp.float32)
        attn = jnp.einsum('nhsk,knd->snhd', probs_b, valset)
        delta = jnp.einsum('snhd,snhd->nhs', grad, attn)
        dprobs = jnp.einsum('snhd,knd->nhsk', grad, valset)
        dscores = (probs * (dprobs - delta[..., None])).astype(jnp.bfloat16).astype(jnp.float32)
        dquery = (jnp.einsum('nhsk,knd->snhd', dscores, keyset) * scale).astype(jnp.bfloat16)
        query_parts.append(dquery.reshape(TOK_DEV, HEADS * HD))
        dkey = jnp.einsum('nhsk,snhd->knd', dscores, query) * scale
        dval = jnp.einsum('nhsk,snhd->knd', probs_b, grad)
        key_parts.append(dkey[nsum:].astype(jnp.bfloat16).reshape(TOK_DEV, KVH * HD))
        value_parts.append(dval[nsum:].astype(jnp.bfloat16).reshape(TOK_DEV, KVH * HD))
        acc_keys = acc_keys + dkey[:nsum]
        acc_vals = acc_vals + dval[:nsum]
    sum_key_grad = acc_keys.reshape(nsum, KVH * HD).astype(jnp.bfloat16)
    sum_value_grad = acc_vals.reshape(nsum, KVH * HD).astype(jnp.bfloat16)
    dims = (((1,), (1,)), ((), ()))
    state = lax.dot_general(sum_key_grad, w_key, dims, preferred_element_type=jnp.float32)
    state = state + lax.dot_general(sum_value_grad, w_value, dims, preferred_element_type=jnp.float32)
    state_grad = (state + summary_grad.astype(jnp.float32)).astype(jnp.bfloat16)
    return (jnp.concatenate(query_parts, 0), jnp.concatenate(key_parts, 0), jnp.concatenate(value_parts, 0), state_grad)
```

```python
import functools
import math

import jax
import jax.numpy as jnp
from jax import lax
from jax.experimental import pallas as pl
from jax.experimental.pallas import tpu as pltpu
from jax.sharding import PartitionSpec as P

HEADS = 64
KVH = 8
HD = 128
GROUP = HEADS // KVH
SCALE = HD ** (-0.5)
LOG2E = math.log2(math.e)
F32 = jnp.float32
BF16 = jnp.bfloat16
LAST = (((1,), (1,)), ((), ()))
VMEM_LIMIT = 48 * 1024 * 1024


def dot(a, b, dims=(((1,), (0,)), ((), ()))):
    return lax.dot_general(a, b, dims, preferred_element_type=F32)


def params(limit=VMEM_LIMIT):
    return pltpu.CompilerParams(vmem_limit_bytes=limit)


def cost(flops, nbytes):
    return pl.CostEstimate(flops=int(flops), bytes_accessed=int(nbytes), transcendentals=0)


def head_lanes(head):
    return pl.ds(pl.multiple_of(head * HD, HD), HD)


def project_kernel(states_ref, wk_ref, wv_ref, out_ref, acc_ref):
    step = pl.program_id(0)
    width = wk_ref.shape[1]

    @pl.when(step == 0)
    def _():
        acc_ref[...] = jnp.zeros_like(acc_ref)

    states = states_ref[...]
    acc_ref[:, :width] += dot(states, wk_ref[...])
    acc_ref[:, width:] += dot(states, wv_ref[...])

    @pl.when(step == pl.num_programs(0) - 1)
    def _():
        out_ref[...] = acc_ref[...].astype(BF16)


def project(states, w_key, w_value, chunk=1024):
    rows, depth = states.shape
    width = w_key.shape[1]
    return pl.pallas_call(
        project_kernel,
        name="project",
        grid=(depth // chunk,),
        in_specs=[
            pl.BlockSpec((rows, chunk), lambda i: (0, i)),
            pl.BlockSpec((chunk, width), lambda i: (i, 0)),
            pl.BlockSpec((chunk, width), lambda i: (i, 0)),
        ],
        out_specs=pl.BlockSpec((rows, 2 * width), lambda i: (0, 0)),
        out_shape=jax.ShapeDtypeStruct((rows, 2 * width), BF16),
        scratch_shapes=[pltpu.VMEM((rows, 2 * width), F32)],
        compiler_params=params(),
        cost_estimate=cost(4 * rows * depth * width, 4 * depth * width),
    )(states, w_key, w_value)


def causal_bias(count):
    key_pos = lax.broadcasted_iota(jnp.int32, (count, count), 0)
    row_pos = lax.broadcasted_iota(jnp.int32, (count, count), 1)
    return jnp.where(key_pos <= row_pos, 0.0, -jnp.inf).astype(F32)


def own_stats_kernel(unroll, q_ref, g_ref, k_ref, v_ref, stats_ref, bias_ref):
    bias_ref[...] = causal_bias(bias_ref.shape[0])
    keys = k_ref[...]
    values = v_ref[...]

    def one(head, _):
        lanes = head_lanes(head)
        scores = dot(keys, q_ref[:, lanes], LAST) * (SCALE * LOG2E) + bias_ref[...]
        top = jnp.max(scores, axis=0, keepdims=True)
        weights = jnp.exp2(scores - top)
        total = jnp.sum(weights, axis=0, keepdims=True)
        dprobs = dot(values, g_ref[:, lanes], LAST)
        mixed = jnp.sum(weights * dprobs, axis=0, keepdims=True)
        stats_ref[head, 0:1, :] = top
        stats_ref[head, 1:2, :] = total
        stats_ref[head, 2:3, :] = mixed
        return 0

    lax.fori_loop(0, GROUP, one, 0, unroll=unroll)


def own_stats(queries, out_grad, keys_own, values_own, unroll):
    rows = queries.shape[0]
    kv_local = keys_own.shape[1] // HD
    heads = kv_local * GROUP
    wide = pl.BlockSpec((rows, GROUP * HD), lambda i: (0, i))
    narrow = pl.BlockSpec((rows, HD), lambda i: (0, i))
    return pl.pallas_call(
        functools.partial(own_stats_kernel, unroll),
        name="own_stats",
        grid=(kv_local,),
        in_specs=[wide, wide, narrow, narrow],
        out_specs=pl.BlockSpec((GROUP, 8, rows), lambda i: (i, 0, 0)),
        out_shape=jax.ShapeDtypeStruct((heads, 8, rows), F32),
        scratch_shapes=[pltpu.VMEM((rows, rows), F32)],
        compiler_params=params(),
        cost_estimate=cost(40 * heads * rows * rows * HD, 4 * rows * heads * HD),
    )(queries, out_grad, keys_own, values_own)


def summary_kernel(
    unroll, count, slots, seg_ref, q_ref, g_ref, k_ref, v_ref, own_ref,
    ds_ref, stats_ref, dk_ref, dv_ref, bias_ref, dk_acc, dv_acc,
):
    position = seg_ref[0]
    rows = q_ref.shape[0]
    padded = k_ref.shape[0]
    row = lax.broadcasted_iota(jnp.int32, (padded, rows), 0)
    bias = jnp.full((padded, rows), -jnp.inf, F32)
    for slot in range(1, slots):
        start = (slot - 1) * count
        shown = jnp.where((position ^ slot) < position, 0.0, -jnp.inf).astype(F32)
        bias = jnp.where((row >= start) & (row < start + count), shown, bias)
    bias_ref[...] = bias
    dk_acc[...] = jnp.zeros_like(dk_acc)
    dv_acc[...] = jnp.zeros_like(dv_acc)
    keys = k_ref[...]
    values = v_ref[...]

    def one(head, _):
        lanes = head_lanes(head)
        query = q_ref[:, lanes]
        grad = g_ref[:, lanes]
        scores = dot(keys, query, LAST) * (SCALE * LOG2E) + bias_ref[...]
        own_top = own_ref[head, 0:1, :]
        top = jnp.maximum(jnp.max(scores, axis=0, keepdims=True), own_top)
        weights = jnp.exp2(scores - top)
        shrink = jnp.exp2(own_top - top)
        total = jnp.sum(weights, axis=0, keepdims=True) + own_ref[head, 1:2, :] * shrink
        inverse = 1.0 / total
        probs = weights * inverse
        dprobs = dot(values, grad, LAST)
        delta = (
            jnp.sum(probs * dprobs, axis=0, keepdims=True)
            + own_ref[head, 2:3, :] * shrink * inverse
        )
        dscores = (probs * (dprobs - delta)).astype(BF16)
        ds_ref[head] = dscores
        stats_ref[head, 0:1, :] = top
        stats_ref[head, 1:2, :] = inverse
        stats_ref[head, 2:3, :] = delta
        dk_acc[...] += dot(dscores, query)
        dv_acc[...] += dot(probs.astype(BF16), grad)
        return 0

    lax.fori_loop(0, GROUP, one, 0, unroll=unroll)
    dk_ref[...] = (dk_acc[...] * SCALE).astype(BF16)
    dv_ref[...] = dv_acc[...].astype(BF16)


def summary_part(position, queries, out_grad, keys, values, own, count, slots, unroll):
    rows = queries.shape[0]
    padded = keys.shape[0]
    kv_local = keys.shape[1] // HD
    heads = kv_local * GROUP
    wide = pl.BlockSpec((rows, GROUP * HD), lambda i, s: (0, i))
    narrow = pl.BlockSpec((padded, HD), lambda i, s: (0, i))
    stats = pl.BlockSpec((GROUP, 8, rows), lambda i, s: (i, 0, 0))
    return pl.pallas_call(
        functools.partial(summary_kernel, unroll, count, slots),
        name="summary_part",
        grid_spec=pltpu.PrefetchScalarGridSpec(
            num_scalar_prefetch=1,
            grid=(kv_local,),
            in_specs=[wide, wide, narrow, narrow, stats],
            out_specs=[
                pl.BlockSpec((GROUP, padded, rows), lambda i, s: (i, 0, 0)),
                stats,
                narrow,
                narrow,
            ],
            scratch_shapes=[
                pltpu.VMEM((padded, rows), F32),
                pltpu.VMEM((padded, HD), F32),
                pltpu.VMEM((padded, HD), F32),
            ],
        ),
        out_shape=[
            jax.ShapeDtypeStruct((heads, padded, rows), BF16),
            jax.ShapeDtypeStruct((heads, 8, rows), F32),
            jax.ShapeDtypeStruct((padded, kv_local * HD), BF16),
            jax.ShapeDtypeStruct((padded, kv_local * HD), BF16),
        ],
        compiler_params=params(),
        cost_estimate=cost(40 * heads * rows * padded * HD, 4 * rows * heads * HD),
    )(position, queries, out_grad, keys, values, own)


def own_grads_kernel(
    unroll, q_ref, g_ref, k_ref, v_ref, sk_ref, ds_ref, stats_ref,
    dq_ref, dk_ref, dv_ref, bias_ref, dk_acc, dv_acc,
):
    bias_ref[...] = causal_bias(bias_ref.shape[0])
    dk_acc[...] = jnp.zeros_like(dk_acc)
    dv_acc[...] = jnp.zeros_like(dv_acc)
    keys = k_ref[...]
    values = v_ref[...]
    keys_t = keys.T
    sum_keys_t = sk_ref[...].T

    def one(head, _):
        lanes = head_lanes(head)
        query = q_ref[:, lanes]
        grad = g_ref[:, lanes]
        scores = dot(keys, query, LAST) * (SCALE * LOG2E) + bias_ref[...]
        top = stats_ref[head, 0:1, :]
        inverse = stats_ref[head, 1:2, :]
        delta = stats_ref[head, 2:3, :]
        probs = jnp.exp2(scores - top) * inverse
        dprobs = dot(values, grad, LAST)
        dscores = (probs * (dprobs - delta)).astype(BF16)
        dk_acc[...] += dot(dscores, query)
        dv_acc[...] += dot(probs.astype(BF16), grad)
        dquery = dot(keys_t, dscores) + dot(sum_keys_t, ds_ref[head])
        dq_ref[:, lanes] = (dquery * SCALE).T.astype(BF16)
        return 0

    lax.fori_loop(0, GROUP, one, 0, unroll=unroll)
    dk_ref[...] = (dk_acc[...] * SCALE).astype(BF16)
    dv_ref[...] = dv_acc[...].astype(BF16)


def own_grads(queries, out_grad, keys_own, values_own, sum_keys, dscores, stats, unroll):
    rows = queries.shape[0]
    padded = sum_keys.shape[0]
    kv_local = keys_own.shape[1] // HD
    heads = kv_local * GROUP
    wide = pl.BlockSpec((rows, GROUP * HD), lambda i: (0, i))
    narrow = pl.BlockSpec((rows, HD), lambda i: (0, i))
    return pl.pallas_call(
        functools.partial(own_grads_kernel, unroll),
        name="own_grads",
        grid=(kv_local,),
        in_specs=[
            wide,
            wide,
            narrow,
            narrow,
            pl.BlockSpec((padded, HD), lambda i: (0, i)),
            pl.BlockSpec((GROUP, padded, rows), lambda i: (i, 0, 0)),
            pl.BlockSpec((GROUP, 8, rows), lambda i: (i, 0, 0)),
        ],
        out_specs=[wide, narrow, narrow],
        out_shape=[
            jax.ShapeDtypeStruct((rows, heads * HD), BF16),
            jax.ShapeDtypeStruct((rows, kv_local * HD), BF16),
            jax.ShapeDtypeStruct((rows, kv_local * HD), BF16),
        ],
        scratch_shapes=[
            pltpu.VMEM((rows, rows), F32),
            pltpu.VMEM((rows, HD), F32),
            pltpu.VMEM((rows, HD), F32),
        ],
        compiler_params=params(),
        cost_estimate=cost(40 * heads * rows * rows * HD, 4 * rows * heads * HD),
    )(queries, out_grad, keys_own, values_own, sum_keys, dscores, stats)


def state_kernel(order_ref, dk_ref, dv_ref, wk_ref, wv_ref, out_ref):
    total = dot(dk_ref[...], wk_ref[...], LAST) + dot(dv_ref[...], wv_ref[...], LAST)
    out_ref[...] = total.astype(BF16)


def state_part(order, emitted_k, emitted_v, w_key, w_value, slices, chunk=1024):
    rows, width = emitted_k.shape
    depth = w_key.shape[0]
    per = depth // slices // chunk
    steps = order.shape[0] * per
    weight = pl.BlockSpec((chunk, width), lambda i, o: (o[i // per] * per + i % per, 0))
    whole = pl.BlockSpec((rows, width), lambda i, o: (0, 0))
    return pl.pallas_call(
        state_kernel,
        name="state_part",
        grid_spec=pltpu.PrefetchScalarGridSpec(
            num_scalar_prefetch=1,
            grid=(steps,),
            in_specs=[whole, whole, weight, weight],
            out_specs=pl.BlockSpec((rows, chunk), lambda i, o: (0, i)),
        ),
        out_shape=jax.ShapeDtypeStruct((rows, steps * chunk), BF16),
        compiler_params=params(),
        cost_estimate=cost(4 * rows * steps * chunk * width, 4 * steps * chunk * width),
    )(order, emitted_k, emitted_v, w_key, w_value)


def exchange(block, axis, size, bit):
    return lax.ppermute(block, axis, [(i, i ^ bit) for i in range(size)])


def per_device(
    queries, keys_own, values_own, out_grad, summary_states, w_key, w_value, summary_grad
):
    rows = queries.shape[0]
    width = keys_own.shape[1]
    count = summary_states.shape[0]
    n_seg = lax.axis_size("seg")
    n_tp = lax.axis_size("tp")
    position = lax.axis_index("seg").astype(jnp.int32).reshape(1)
    mine = lax.axis_index("tp").astype(jnp.int32)
    unroll = GROUP if n_seg <= 8 else 1

    projected = project(summary_states, w_key, w_value)
    own = own_stats(queries, out_grad, keys_own, values_own, unroll)

    chunks = {0: projected}
    bit = n_seg // 2
    while bit:
        held = sorted(chunks)
        got = exchange(jnp.concatenate([chunks[j] for j in held], 0), "seg", n_seg, bit)
        for at, j in enumerate(held):
            chunks[j ^ bit] = got[at * count : (at + 1) * count]
        bit //= 2
    shown = (n_seg - 1) * count
    padded = -(-shown // 16) * 16
    tail = [jnp.zeros((padded - shown, 2 * width), BF16)] if padded > shown else []
    gathered = jnp.concatenate([chunks[j] for j in range(1, n_seg)] + tail, 0)
    sum_keys, sum_values = gathered[:, :width], gathered[:, width:]

    dscores, stats, dk, dv = summary_part(
        position, queries, out_grad, sum_keys, sum_values, own, count, n_seg, unroll
    )

    both = jnp.concatenate([dk, dv], 1)
    parts = {j: both[(j - 1) * count : j * count].astype(F32) for j in range(1, n_seg)}
    bit = 1
    while bit < n_seg:
        sent = sorted(j for j in parts if j & bit)
        block = jnp.concatenate([parts.pop(j).astype(BF16) for j in sent], 0)
        got = exchange(block, "seg", n_seg, bit).astype(F32)
        for at, j in enumerate(sent):
            piece = got[at * count : (at + 1) * count]
            parts[j ^ bit] = parts[j ^ bit] + piece if j ^ bit in parts else piece
        bit *= 2
    emitted = parts[0].astype(BF16)

    query_grad, key_grad, value_grad = own_grads(
        queries, out_grad, keys_own, values_own, sum_keys, dscores, stats, unroll
    )

    slice_width = w_key.shape[0] // n_tp
    far = list(range(n_tp - 1, 1, -1))
    near = [1, 0] if n_tp > 1 else [0]
    terms = {}
    for group in (far, near):
        if group:
            order = jnp.stack([mine ^ j for j in group])
            block = state_part(
                order, emitted[:, :width], emitted[:, width:], w_key, w_value, n_tp
            )
            for at, j in enumerate(group):
                terms[j] = block[:, at * slice_width : (at + 1) * slice_width].astype(F32)
    bit = 1
    while bit < n_tp:
        for group in ([j for j in terms if j & bit and j > bit], [bit]):
            if not group:
                continue
            block = jnp.concatenate([terms.pop(j).astype(BF16) for j in group], 1)
            got = exchange(block, "tp", n_tp, bit).astype(F32)
            for at, j in enumerate(group):
                terms[j ^ bit] += got[:, at * slice_width : (at + 1) * slice_width]
        bit *= 2
    state_grad = (terms[0] + summary_grad.astype(F32)).astype(BF16)
    return (query_grad, key_grad, value_grad, state_grad)


def solution(mesh):
    placed = (
        P("seg", "tp"),
        P("seg", "tp"),
        P("seg", "tp"),
        P("seg", "tp"),
        P("seg", None),
        P(None, "tp"),
        P(None, "tp"),
        P("seg", "tp"),
    )
    return jax.shard_map(
        per_device,
        mesh=mesh,
        in_specs=placed,
        out_specs=(P("seg", "tp"), P("seg", "tp"), P("seg", "tp"), P("seg", "tp")),
        check_vma=False,
    )
```

```python
import functools
import math

import jax
import jax.numpy as jnp
from jax import lax
from jax.experimental import pallas as pl
from jax.experimental.pallas import tpu as pltpu
from jax.sharding import PartitionSpec as P

HEADS = 64
KVH = 8
HD = 128
GROUP = HEADS // KVH
SCALE = HD ** (-0.5)
SCALE2 = SCALE * math.log2(math.e)
F32 = jnp.float32
BF16 = jnp.bfloat16
MIB = 1024 * 1024
LAST = (((1,), (1,)), ((), ()))
VMEM = pl.BlockSpec(memory_space=pltpu.VMEM)
ANY = pl.BlockSpec(memory_space=pl.ANY)
HBM = pl.BlockSpec(memory_space=pltpu.HBM)


def dot(a, b, dims=(((1,), (0,)), ((), ()))):
    return lax.dot_general(a, b, dims, preferred_element_type=F32)


def params(mib):
    return pltpu.CompilerParams(vmem_limit_bytes=mib * MIB)


def cost(flops, nbytes):
    return pl.CostEstimate(flops=int(flops), bytes_accessed=int(nbytes), transcendentals=0)


def shape(dims, dtype=BF16):
    return jax.ShapeDtypeStruct(dims, dtype)


def lanes(index):
    return slice(index * HD, (index + 1) * HD)


def round_up(value, unit):
    return -(-value // unit) * unit


def project_kernel(
    pieces, states_hbm, wk_hbm, wv_hbm, out_ref, wk_ref, wv_ref, states_ref, sems
):
    width = wk_ref.shape[1]
    chunk = wk_ref.shape[0] // pieces
    states_copy = pltpu.make_async_copy(states_hbm, states_ref, sems.at[2 * pieces])
    states_copy.start()
    copies = []
    for at in range(pieces):
        rows = pl.ds(at * chunk, chunk)
        pair = (
            pltpu.make_async_copy(wk_hbm.at[rows], wk_ref.at[rows], sems.at[2 * at]),
            pltpu.make_async_copy(wv_hbm.at[rows], wv_ref.at[rows], sems.at[2 * at + 1]),
        )
        for copy in pair:
            copy.start()
        copies.append(pair)
    states_copy.wait()
    keys = values = None
    for at, (key_copy, value_copy) in enumerate(copies):
        rows = slice(at * chunk, (at + 1) * chunk)
        states = states_ref[:, rows]
        key_copy.wait()
        term = dot(states, wk_ref[rows, :])
        keys = term if keys is None else keys + term
        value_copy.wait()
        term = dot(states, wv_ref[rows, :])
        values = term if values is None else values + term
    out_ref[:, :width] = keys.astype(BF16)
    out_ref[:, width:] = values.astype(BF16)


def project(states, w_key, w_value, pieces=8):
    rows, depth = states.shape
    width = w_key.shape[1]
    return pl.pallas_call(
        functools.partial(project_kernel, pieces),
        name="project",
        in_specs=[HBM] * 3,
        out_specs=VMEM,
        out_shape=shape((rows, 2 * width)),
        scratch_shapes=[
            pltpu.VMEM(w_key.shape, BF16),
            pltpu.VMEM(w_value.shape, BF16),
            pltpu.VMEM((rows, depth), BF16),
            pltpu.SemaphoreType.DMA((2 * pieces + 1,)),
        ],
        compiler_params=params(12),
        cost_estimate=cost(4 * rows * depth * width, 8 * depth * width),
    )(*(pltpu.with_memory_space_constraint(x, pltpu.HBM) for x in (states, w_key, w_value)))


def causal_bias(count):
    key_pos = lax.broadcasted_iota(jnp.int32, (count, count), 0)
    row_pos = lax.broadcasted_iota(jnp.int32, (count, count), 1)
    return jnp.where(key_pos <= row_pos, 0.0, -jnp.inf).astype(F32)


def own_stats_kernel(q_ref, g_ref, k_ref, v_ref, stats_ref, bias_ref):
    bias_ref[...] = causal_bias(bias_ref.shape[0])
    for kv in range(k_ref.shape[1] // HD):
        keys = k_ref[:, lanes(kv)]
        values = v_ref[:, lanes(kv)]
        for head in range(kv * GROUP, (kv + 1) * GROUP):
            scores = dot(keys, q_ref[:, lanes(head)], LAST) * SCALE2 + bias_ref[...]
            top = jnp.max(scores, axis=0, keepdims=True)
            weights = jnp.exp2(scores - top)
            dprobs = dot(values, g_ref[:, lanes(head)], LAST)
            stats_ref[head, 0:1, :] = top
            stats_ref[head, 1:2, :] = jnp.sum(weights, axis=0, keepdims=True)
            stats_ref[head, 2:3, :] = jnp.sum(weights * dprobs, axis=0, keepdims=True)


def own_stats(queries, out_grad, keys_own, values_own, held):
    rows = queries.shape[0]
    heads = queries.shape[1] // HD
    return pl.pallas_call(
        own_stats_kernel,
        name="own_stats",
        in_specs=[VMEM] * 4,
        out_specs=VMEM,
        out_shape=shape((heads, 8, rows), F32),
        scratch_shapes=[pltpu.VMEM((rows, rows), F32)],
        compiler_params=params(12),
        cost_estimate=cost(20 * heads * rows * rows * HD, 4 * rows * heads * HD),
    )(queries, out_grad, keys_own, values_own, *held)


def summary_kernel(
    count, slots, seg_ref, q_ref, g_ref, odd_ref, even_ref, own_ref,
    ds_ref, stats_ref, keys_ref, odd_grad_ref, even_grad_ref, bias_ref, both_ref,
):
    position = seg_ref[0]
    rows = q_ref.shape[0]
    padded = both_ref.shape[0]
    split = odd_ref.shape[0]
    shown = split + even_ref.shape[0]
    kv_local = keys_ref.shape[1] // HD
    width = kv_local * HD

    row = lax.broadcasted_iota(jnp.int32, (padded, rows), 0)
    bias = jnp.full((padded, rows), -jnp.inf, F32)
    for at, slot in enumerate(slots):
        level = jnp.where((position ^ slot) < position, 0.0, -jnp.inf).astype(F32)
        bias = jnp.where((row >= at * count) & (row < (at + 1) * count), level, bias)
    bias_ref[...] = bias
    if padded > shown:
        tail = round_up(shown, 8) - 8
        both_ref[tail:, :] = jnp.zeros((padded - tail, 2 * width), F32)
    both_ref[:split, :] = odd_ref[...].astype(F32)
    both_ref[split:shown, :] = even_ref[...].astype(F32)
    keys_ref[...] = both_ref[:, :width].astype(BF16)

    for kv in range(kv_local):
        keys = keys_ref[:, lanes(kv)]
        values = both_ref[:, width + kv * HD : width + (kv + 1) * HD].astype(BF16)
        heads = range(kv * GROUP, (kv + 1) * GROUP)
        all_dscores, all_probs = [], []
        for head in heads:
            scores = dot(keys, q_ref[:, lanes(head)], LAST) * SCALE2 + bias_ref[...]
            own_top = own_ref[head, 0:1, :]
            top = jnp.maximum(jnp.max(scores, axis=0, keepdims=True), own_top)
            weights = jnp.exp2(scores - top)
            shrink = jnp.exp2(own_top - top)
            total = jnp.sum(weights, axis=0, keepdims=True) + own_ref[head, 1:2, :] * shrink
            inverse = 1.0 / total
            probs = weights * inverse
            dprobs = dot(values, g_ref[:, lanes(head)], LAST)
            delta = jnp.sum(probs * dprobs, axis=0, keepdims=True)
            delta = delta + own_ref[head, 2:3, :] * shrink * inverse
            dscores = (probs * (dprobs - delta)).astype(BF16)
            ds_ref[head] = dscores
            all_dscores.append(dscores)
            all_probs.append(probs.astype(BF16))
            stats_ref[head, 0:1, :] = top
            stats_ref[head, 1:2, :] = inverse
            stats_ref[head, 2:3, :] = delta
        queries = jnp.concatenate([q_ref[:, lanes(head)] for head in heads], 0)
        grads = jnp.concatenate([g_ref[:, lanes(head)] for head in heads], 0)
        key_part = dot(jnp.concatenate(all_dscores, 1), queries) * SCALE
        value_part = dot(jnp.concatenate(all_probs, 1), grads)
        both_ref[:, lanes(kv)] = key_part
        both_ref[:, width + kv * HD : width + (kv + 1) * HD] = value_part
    odd_grad_ref[...] = both_ref[:split, :].astype(BF16)
    even_grad_ref[...] = both_ref[split:shown, :]


def summary_part(position, queries, out_grad, odd, even, own, held, count, slots):
    rows = queries.shape[0]
    width = odd.shape[1] // 2
    heads = queries.shape[1] // HD
    padded = round_up(odd.shape[0] + even.shape[0], 16)
    return pl.pallas_call(
        functools.partial(summary_kernel, count, slots),
        name="summary_part",
        in_specs=[pl.BlockSpec(memory_space=pltpu.SMEM)] + [VMEM] * 5,
        out_specs=[VMEM] * 5,
        out_shape=[
            shape((heads, padded, rows)),
            shape((heads, 8, rows), F32),
            shape((padded, width)),
            shape(odd.shape),
            shape(even.shape, F32),
        ],
        scratch_shapes=[
            pltpu.VMEM((padded, rows), F32),
            pltpu.VMEM((padded, 2 * width), F32),
        ],
        compiler_params=params(16 if padded <= 512 else 48),
        cost_estimate=cost(40 * heads * rows * padded * HD, 4 * rows * heads * HD),
    )(position, queries, out_grad, odd, even, own, *held)


def own_grads_kernel(
    kv, q_ref, g_ref, k_ref, v_ref, sk_ref, ds_ref, stats_ref, *rest
):
    dq_out, dk_ref, dv_ref, bias_ref, dq_ref, sem = rest[-6:]
    bias_ref[...] = causal_bias(bias_ref.shape[0])
    keys = k_ref[:, lanes(kv)]
    values = v_ref[:, lanes(kv)]
    keys_t = jnp.concatenate([sk_ref[:, lanes(kv)], keys], 0).T
    heads = range(kv * GROUP, (kv + 1) * GROUP)
    all_dscores, all_probs = [], []
    for at, head in enumerate(heads):
        scores = dot(keys, q_ref[:, lanes(head)], LAST) * SCALE2 + bias_ref[...]
        probs = jnp.exp2(scores - stats_ref[head, 0:1, :]) * stats_ref[head, 1:2, :]
        dprobs = dot(values, g_ref[:, lanes(head)], LAST)
        dscores = (probs * (dprobs - stats_ref[head, 2:3, :])).astype(BF16)
        all_dscores.append(dscores)
        all_probs.append(probs.astype(BF16))
        dquery = dot(keys_t, jnp.concatenate([ds_ref[head], dscores], 0))
        dq_ref[:, lanes(at)] = (dquery * SCALE).T.astype(BF16)
    columns = pl.ds(kv * GROUP * HD, GROUP * HD)
    copy = pltpu.make_async_copy(dq_ref, dq_out.at[:, columns], sem)
    copy.start()
    queries = jnp.concatenate([q_ref[:, lanes(head)] for head in heads], 0)
    grads = jnp.concatenate([g_ref[:, lanes(head)] for head in heads], 0)
    dk_ref[...] = (dot(jnp.concatenate(all_dscores, 1), queries) * SCALE).astype(BF16)
    dv_ref[...] = dot(jnp.concatenate(all_probs, 1), grads).astype(BF16)
    copy.wait()


def own_grads(kv, queries, out_grad, keys_own, values_own, sum_keys, dscores, stats, held, earlier):
    rows = queries.shape[0]
    heads = queries.shape[1] // HD
    padded = sum_keys.shape[0]
    operands = [queries, out_grad, keys_own, values_own, sum_keys, dscores, stats, *held]
    in_specs = [VMEM] * 7
    aliases = {}
    if earlier is not None:
        operands.append(earlier)
        in_specs.append(HBM)
        aliases = {7: 0}
    return pl.pallas_call(
        functools.partial(own_grads_kernel, kv),
        name="own_grads",
        in_specs=in_specs,
        out_specs=[HBM, VMEM, VMEM],
        out_shape=[shape((rows, heads * HD)), shape((rows, HD)), shape((rows, HD))],
        input_output_aliases=aliases,
        scratch_shapes=[
            pltpu.VMEM((rows, rows), F32),
            pltpu.VMEM((rows, GROUP * HD), BF16),
            pltpu.SemaphoreType.DMA,
        ],
        compiler_params=params(16 if padded <= 512 else 32),
        cost_estimate=cost(20 * heads * rows * rows * HD, 4 * rows * heads * HD),
    )(*operands)


def state_kernel(chunk, group, mine_ref, emitted_ref, wk_ref, wv_ref, *out_refs):
    width = wk_ref.shape[1]
    keys = emitted_ref[:, :width]
    values = emitted_ref[:, width:]
    wide = out_refs[0].shape[1]
    for at, out_ref in enumerate(out_refs):
        for step in range(wide // chunk):
            rows = pl.ds(pl.multiple_of((mine_ref[0] ^ group[at]) * wide + step * chunk, chunk), chunk)
            total = dot(keys, wk_ref[rows, :], LAST) + dot(values, wv_ref[rows, :], LAST)
            out_ref[:, step * chunk : (step + 1) * chunk] = total.astype(BF16)


def state_part(mine, emitted, w_key, w_value, wide, group, chunk=512):
    rows = emitted.shape[0]
    width = w_key.shape[1]
    count = len(group)
    return pl.pallas_call(
        functools.partial(state_kernel, chunk, group),
        name="state_part",
        in_specs=[pl.BlockSpec(memory_space=pltpu.SMEM)] + [VMEM] * 3,
        out_specs=[VMEM] * count,
        out_shape=[shape((rows, wide))] * count,
        compiler_params=params(14),
        cost_estimate=cost(4 * rows * count * wide * width, 4 * count * wide * width),
    )(mine, emitted, w_key, w_value)


def exchange(block, axis, size, key):
    return lax.ppermute(block, axis, [(i, i ^ key) for i in range(size)])


def per_device(
    queries, keys_own, values_own, out_grad, summary_states, w_key, w_value, summary_grad
):
    kv_local = keys_own.shape[1] // HD
    count = summary_states.shape[0]
    n_seg = lax.axis_size("seg")
    n_tp = lax.axis_size("tp")
    position = lax.axis_index("seg").astype(jnp.int32).reshape(1)
    mine = lax.axis_index("tp").astype(jnp.int32).reshape(1)

    projected = project(summary_states, w_key, w_value)
    held = ()
    own = own_stats(queries, out_grad, keys_own, values_own, held)

    evens = list(range(n_seg - 2, 0, -2))
    odds = [j + 1 for j in evens] + [1]
    chunks = {j: exchange(projected, "seg", n_seg, j) for j in evens}
    even = jnp.concatenate([chunks[j] for j in evens], 0)
    odd = jnp.concatenate(
        [exchange(even, "seg", n_seg, 1), exchange(projected, "seg", n_seg, 1)], 0
    )

    dscores, stats, sum_keys, odd_grad, even_grad = summary_part(
        position, queries, out_grad, odd, even, own, held, count, odds + evens
    )

    query_grad = None
    key_blocks, value_blocks = [], []

    def own_part(kv, earlier):
        query_grad, key_block, value_block = own_grads(
            kv, queries, out_grad, keys_own, values_own, sum_keys, dscores, stats, held, earlier
        )
        key_blocks.append(key_block)
        value_blocks.append(value_block)
        return query_grad

    got = exchange(odd_grad, "seg", n_seg, 1)
    query_grad = own_part(0, None)
    got, query_grad = lax.optimization_barrier((got, query_grad))
    got = got.astype(F32)
    emitted = got[len(evens) * count :]
    blocks = []
    for at, j in enumerate(evens):
        rows = slice(at * count, (at + 1) * count)
        block = (even_grad[rows] + got[rows]).astype(BF16)
        blocks.append(exchange(block, "seg", n_seg, j))
    for kv in range(1, kv_local):
        query_grad = own_part(kv, query_grad)
    blocks, query_grad = lax.optimization_barrier((blocks, query_grad))
    for block in blocks:
        emitted = emitted + block.astype(F32)
    emitted = emitted.astype(BF16)
    key_grad = jnp.concatenate(key_blocks, 1)
    value_grad = jnp.concatenate(value_blocks, 1)

    wide = w_key.shape[0] // n_tp
    terms = {}
    for group in (list(range(n_tp - 1, 1, -1)), [1, 0]):
        terms.update(zip(group, state_part(mine, emitted, w_key, w_value, wide, group)))
    bit = 1
    while bit < n_tp:
        for j in sorted((j for j in terms if j & bit), reverse=True):
            got = exchange(terms.pop(j).astype(BF16), "tp", n_tp, bit)
            terms[j ^ bit] = terms[j ^ bit].astype(F32) + got.astype(F32)
        bit *= 2
    state_grad = (terms[0] + summary_grad.astype(F32)).astype(BF16)
    return (query_grad, key_grad, value_grad, state_grad)


def solution(mesh):
    placed = (
        P("seg", "tp"),
        P("seg", "tp"),
        P("seg", "tp"),
        P("seg", "tp"),
        P("seg", None),
        P(None, "tp"),
        P(None, "tp"),
        P("seg", "tp"),
    )
    return jax.shard_map(
        per_device,
        mesh=mesh,
        in_specs=placed,
        out_specs=(P("seg", "tp"), P("seg", "tp"), P("seg", "tp"), P("seg", "tp")),
        check_vma=False,
    )
```

```python
import functools
import math

import jax
import jax.numpy as jnp
from jax import lax
from jax.experimental import pallas as pl
from jax.experimental.pallas import tpu as pltpu
from jax.sharding import PartitionSpec as P

HEADS = 64
KVH = 8
HD = 128
GROUP = HEADS // KVH
SCALE = HD ** (-0.5)
SCALE2 = SCALE * math.log2(math.e)
F32 = jnp.float32
BF16 = jnp.bfloat16
MIB = 1024 * 1024
LAST = (((1,), (1,)), ((), ()))
VMEM = pl.BlockSpec(memory_space=pltpu.VMEM)
ANY = pl.BlockSpec(memory_space=pl.ANY)
SMEM = pl.BlockSpec(memory_space=pltpu.SMEM)
HBM = pl.BlockSpec(memory_space=pltpu.HBM)


def dot(a, b, dims=(((1,), (0,)), ((), ()))):
    return lax.dot_general(a, b, dims, preferred_element_type=F32)


def params(mib):
    return pltpu.CompilerParams(vmem_limit_bytes=mib * MIB)


def cost(flops, nbytes):
    return pl.CostEstimate(flops=int(flops), bytes_accessed=int(nbytes), transcendentals=0)


def shape(dims, dtype=BF16):
    return jax.ShapeDtypeStruct(dims, dtype)


def lanes(index):
    return slice(index * HD, (index + 1) * HD)


def round_up(value, unit):
    return -(-value // unit) * unit


def project_kernel(
    pieces, states_hbm, wk_hbm, wv_hbm, out_ref, wk_ref, wv_ref, states_ref, sems
):
    width = wk_ref.shape[1]
    chunk = wk_ref.shape[0] // pieces
    states_copy = pltpu.make_async_copy(states_hbm, states_ref, sems.at[2 * pieces])
    states_copy.start()
    copies = []
    for at in range(pieces):
        rows = pl.ds(at * chunk, chunk)
        pair = (
            pltpu.make_async_copy(wk_hbm.at[rows], wk_ref.at[rows], sems.at[2 * at]),
            pltpu.make_async_copy(wv_hbm.at[rows], wv_ref.at[rows], sems.at[2 * at + 1]),
        )
        for copy in pair:
            copy.start()
        copies.append(pair)
    states_copy.wait()
    keys = values = None
    for at, (key_copy, value_copy) in enumerate(copies):
        rows = slice(at * chunk, (at + 1) * chunk)
        states = states_ref[:, rows]
        key_copy.wait()
        term = dot(states, wk_ref[rows, :])
        keys = term if keys is None else keys + term
        value_copy.wait()
        term = dot(states, wv_ref[rows, :])
        values = term if values is None else values + term
    out_ref[:, :width] = keys.astype(BF16)
    out_ref[:, width:] = values.astype(BF16)


def project(states, w_key, w_value, pieces=8):
    rows, depth = states.shape
    width = w_key.shape[1]
    return pl.pallas_call(
        functools.partial(project_kernel, pieces),
        name="project",
        in_specs=[HBM] * 3,
        out_specs=VMEM,
        out_shape=shape((rows, 2 * width)),
        scratch_shapes=[
            pltpu.VMEM(w_key.shape, BF16),
            pltpu.VMEM(w_value.shape, BF16),
            pltpu.VMEM((rows, depth), BF16),
            pltpu.SemaphoreType.DMA((2 * pieces + 1,)),
        ],
        compiler_params=params(12),
        cost_estimate=cost(4 * rows * depth * width, 8 * depth * width),
    )(*(pltpu.with_memory_space_constraint(x, pltpu.HBM) for x in (states, w_key, w_value)))


def causal_bias(count):
    key_pos = lax.broadcasted_iota(jnp.int32, (count, count), 0)
    row_pos = lax.broadcasted_iota(jnp.int32, (count, count), 1)
    return jnp.where(key_pos <= row_pos, 0.0, -jnp.inf).astype(F32)


def slot_bias(position, slots, count, dims):
    row = lax.broadcasted_iota(jnp.int32, dims, 0)
    bias = jnp.full(dims, -jnp.inf, F32)
    for at, slot in enumerate(slots):
        level = jnp.where((position ^ slot) < position, 0.0, -jnp.inf).astype(F32)
        bias = jnp.where((row >= at * count) & (row < (at + 1) * count), level, bias)
    return bias


def fill_padded(wide_ref, rows_ref):
    shown = rows_ref.shape[0]
    padded = wide_ref.shape[0]
    tail = shown // 8 * 8
    if padded > tail:
        wide_ref[tail:, :] = jnp.zeros((padded - tail, wide_ref.shape[1]), F32)
    wide_ref[:shown, :] = rows_ref[...].astype(F32)


def own_stats_kernel(q_ref, g_ref, k_ref, v_ref, stats_ref, bias_ref):
    bias_ref[...] = causal_bias(bias_ref.shape[0])
    for kv in range(k_ref.shape[1] // HD):
        keys = k_ref[:, lanes(kv)]
        values = v_ref[:, lanes(kv)]
        for head in range(kv * GROUP, (kv + 1) * GROUP):
            scores = dot(keys, q_ref[:, lanes(head)], LAST) * SCALE2 + bias_ref[...]
            top = jnp.max(scores, axis=0, keepdims=True)
            weights = jnp.exp2(scores - top)
            dprobs = dot(values, g_ref[:, lanes(head)], LAST)
            stats_ref[head, 0:1, :] = top
            stats_ref[head, 1:2, :] = jnp.sum(weights, axis=0, keepdims=True)
            stats_ref[head, 2:3, :] = jnp.sum(weights * dprobs, axis=0, keepdims=True)


def own_stats(queries, out_grad, keys_own, values_own):
    rows = queries.shape[0]
    heads = queries.shape[1] // HD
    return pl.pallas_call(
        own_stats_kernel,
        name="own_stats",
        in_specs=[VMEM] * 4,
        out_specs=VMEM,
        out_shape=shape((heads, 8, rows), F32),
        scratch_shapes=[pltpu.VMEM((rows, rows), F32)],
        compiler_params=params(12),
        cost_estimate=cost(20 * heads * rows * rows * HD, 4 * rows * heads * HD),
    )(queries, out_grad, keys_own, values_own)


def even_stats_kernel(
    count, evens, odds, seg_ref, q_ref, g_ref, even_ref, own_ref,
    stats_ref, even_bias_ref, odd_bias_ref, wide_ref,
):
    position = seg_ref[0]
    width = even_ref.shape[1] // 2
    even_bias_ref[...] = slot_bias(position, evens, count, even_bias_ref.shape)
    odd_bias_ref[...] = slot_bias(position, odds, count, odd_bias_ref.shape)
    fill_padded(wide_ref, even_ref)
    for kv in range(width // HD):
        keys = wide_ref[:, lanes(kv)].astype(BF16)
        values = wide_ref[:, lanes(width // HD + kv)].astype(BF16)
        for head in range(kv * GROUP, (kv + 1) * GROUP):
            scores = dot(keys, q_ref[:, lanes(head)], LAST) * SCALE2 + even_bias_ref[...]
            own_top = own_ref[head, 0:1, :]
            top = jnp.maximum(jnp.max(scores, axis=0, keepdims=True), own_top)
            weights = jnp.exp2(scores - top)
            shrink = jnp.exp2(own_top - top)
            dprobs = dot(values, g_ref[:, lanes(head)], LAST)
            total = jnp.sum(weights, axis=0, keepdims=True)
            mixed = jnp.sum(weights * dprobs, axis=0, keepdims=True)
            stats_ref[head, 0:1, :] = top
            stats_ref[head, 1:2, :] = total + own_ref[head, 1:2, :] * shrink
            stats_ref[head, 2:3, :] = mixed + own_ref[head, 2:3, :] * shrink


def even_stats(position, queries, out_grad, even, own, count, evens, odds):
    rows = queries.shape[0]
    heads = queries.shape[1] // HD
    padded = round_up(even.shape[0], 16)
    return pl.pallas_call(
        functools.partial(even_stats_kernel, count, evens, odds),
        name="even_stats",
        in_specs=[SMEM] + [VMEM] * 4,
        out_specs=[VMEM] * 3,
        out_shape=[
            shape((heads, 8, rows), F32),
            shape((padded, rows), F32),
            shape((round_up(len(odds) * count, 16), rows), F32),
        ],
        scratch_shapes=[pltpu.VMEM((padded, even.shape[1]), F32)],
        compiler_params=params(12 if padded <= 512 else 32),
        cost_estimate=cost(20 * heads * rows * padded * HD, 4 * rows * heads * HD),
    )(position, queries, out_grad, even, own)


def slots_kernel(
    last, q_ref, g_ref, slots_ref, before_ref, bias_ref,
    ds_ref, stats_ref, keys_ref, grad_ref, wide_ref,
):
    shown = slots_ref.shape[0]
    kv_local = keys_ref.shape[1] // HD
    width = kv_local * HD
    fill_padded(wide_ref, slots_ref)
    keys_ref[...] = wide_ref[:, :width].astype(BF16)
    for kv in range(kv_local):
        keys = keys_ref[:, lanes(kv)]
        values = wide_ref[:, lanes(kv_local + kv)].astype(BF16)
        heads = range(kv * GROUP, (kv + 1) * GROUP)
        all_dscores, all_probs = [], []
        for head in heads:
            scores = dot(keys, q_ref[:, lanes(head)], LAST) * SCALE2 + bias_ref[...]
            dprobs = dot(values, g_ref[:, lanes(head)], LAST)
            old_top = before_ref[head, 0:1, :]
            if last:
                top = jnp.maximum(jnp.max(scores, axis=0, keepdims=True), old_top)
                weights = jnp.exp2(scores - top)
                shrink = jnp.exp2(old_top - top)
                total = jnp.sum(weights, axis=0, keepdims=True)
                inverse = 1.0 / (total + before_ref[head, 1:2, :] * shrink)
                mixed = jnp.sum(weights * dprobs, axis=0, keepdims=True)
                delta = (mixed + before_ref[head, 2:3, :] * shrink) * inverse
                probs = weights * inverse
                stats_ref[head, 0:1, :] = top
                stats_ref[head, 1:2, :] = inverse
                stats_ref[head, 2:3, :] = delta
            else:
                probs = jnp.exp2(scores - old_top) * before_ref[head, 1:2, :]
                delta = before_ref[head, 2:3, :]
            dscores = (probs * (dprobs - delta)).astype(BF16)
            ds_ref[head] = dscores
            all_dscores.append(dscores)
            all_probs.append(probs.astype(BF16))
        queries = jnp.concatenate([q_ref[:, lanes(head)] for head in heads], 0)
        grads = jnp.concatenate([g_ref[:, lanes(head)] for head in heads], 0)
        key_part = dot(jnp.concatenate(all_dscores, 1), queries) * SCALE
        value_part = dot(jnp.concatenate(all_probs, 1), grads)
        grad_ref[:, lanes(kv)] = key_part[:shown].astype(grad_ref.dtype)
        grad_ref[:, lanes(kv_local + kv)] = value_part[:shown].astype(grad_ref.dtype)
    if not last:
        stats_ref[...] = jnp.zeros_like(stats_ref)


def slots_part(last, queries, out_grad, slots, before, bias):
    rows = queries.shape[0]
    shown, width = slots.shape[0], slots.shape[1] // 2
    heads = queries.shape[1] // HD
    padded = round_up(shown, 16)
    return pl.pallas_call(
        functools.partial(slots_kernel, last),
        name="odd_slots" if last else "even_slots",
        in_specs=[VMEM] * 5,
        out_specs=[VMEM] * 4,
        out_shape=[
            shape((heads, padded, rows)),
            shape((heads, 8, rows) if last else (8, HD), F32),
            shape((padded, width)),
            shape(slots.shape, BF16 if last else F32),
        ],
        scratch_shapes=[pltpu.VMEM((padded, 2 * width), F32)],
        compiler_params=params(16 if padded <= 512 else 40),
        cost_estimate=cost(30 * heads * rows * padded * HD, 4 * rows * heads * HD),
    )(queries, out_grad, slots, before, bias)


def own_grads_kernel(
    kv, q_ref, g_ref, k_ref, v_ref, ok_ref, ek_ref, ods_ref, eds_ref, stats_ref, *rest
):
    dq_out, dk_ref, dv_ref, bias_ref, dq_ref, sem = rest[-6:]
    bias_ref[...] = causal_bias(bias_ref.shape[0])
    keys = k_ref[:, lanes(kv)]
    values = v_ref[:, lanes(kv)]
    keys_t = jnp.concatenate([ok_ref[:, lanes(kv)], ek_ref[:, lanes(kv)], keys], 0).T
    heads = range(kv * GROUP, (kv + 1) * GROUP)
    all_dscores, all_probs = [], []
    for at, head in enumerate(heads):
        scores = dot(keys, q_ref[:, lanes(head)], LAST) * SCALE2 + bias_ref[...]
        probs = jnp.exp2(scores - stats_ref[head, 0:1, :]) * stats_ref[head, 1:2, :]
        dprobs = dot(values, g_ref[:, lanes(head)], LAST)
        dscores = (probs * (dprobs - stats_ref[head, 2:3, :])).astype(BF16)
        all_dscores.append(dscores)
        all_probs.append(probs.astype(BF16))
        dquery = dot(keys_t, jnp.concatenate([ods_ref[head], eds_ref[head], dscores], 0))
        dq_ref[:, lanes(at)] = (dquery * SCALE).T.astype(BF16)
    columns = pl.ds(kv * GROUP * HD, GROUP * HD)
    copy = pltpu.make_async_copy(dq_ref, dq_out.at[:, columns], sem)
    copy.start()
    queries = jnp.concatenate([q_ref[:, lanes(head)] for head in heads], 0)
    grads = jnp.concatenate([g_ref[:, lanes(head)] for head in heads], 0)
    dk_ref[...] = (dot(jnp.concatenate(all_dscores, 1), queries) * SCALE).astype(BF16)
    dv_ref[...] = dot(jnp.concatenate(all_probs, 1), grads).astype(BF16)
    copy.wait()


def own_grads(kv, operands, earlier):
    queries, odd_keys, even_keys = operands[0], operands[4], operands[5]
    rows = queries.shape[0]
    heads = queries.shape[1] // HD
    padded = odd_keys.shape[0] + even_keys.shape[0]
    in_specs = [VMEM] * len(operands)
    aliases = {}
    if earlier is not None:
        aliases = {len(operands): 0}
        operands = [*operands, earlier]
        in_specs.append(HBM)
    return pl.pallas_call(
        functools.partial(own_grads_kernel, kv),
        name="own_grads",
        in_specs=in_specs,
        out_specs=[HBM, VMEM, VMEM],
        out_shape=[shape((rows, heads * HD)), shape((rows, HD)), shape((rows, HD))],
        input_output_aliases=aliases,
        scratch_shapes=[
            pltpu.VMEM((rows, rows), F32),
            pltpu.VMEM((rows, GROUP * HD), BF16),
            pltpu.SemaphoreType.DMA,
        ],
        compiler_params=params(16 if padded <= 512 else 32),
        cost_estimate=cost(20 * heads * rows * rows * HD, 4 * rows * heads * HD),
    )(*operands)


def state_kernel(chunk, group, mine_ref, emitted_ref, wk_ref, wv_ref, *out_refs):
    width = wk_ref.shape[1]
    keys = emitted_ref[:, :width]
    values = emitted_ref[:, width:]
    wide = out_refs[0].shape[1]
    for at, out_ref in enumerate(out_refs):
        for step in range(wide // chunk):
            rows = pl.ds(pl.multiple_of((mine_ref[0] ^ group[at]) * wide + step * chunk, chunk), chunk)
            total = dot(keys, wk_ref[rows, :], LAST) + dot(values, wv_ref[rows, :], LAST)
            out_ref[:, step * chunk : (step + 1) * chunk] = total.astype(BF16)


def state_part(mine, emitted, w_key, w_value, wide, group, chunk=512):
    rows = emitted.shape[0]
    width = w_key.shape[1]
    count = len(group)
    return pl.pallas_call(
        functools.partial(state_kernel, chunk, group),
        name="state_part",
        in_specs=[SMEM] + [VMEM] * 3,
        out_specs=[VMEM] * count,
        out_shape=[shape((rows, wide))] * count,
        compiler_params=params(14),
        cost_estimate=cost(4 * rows * count * wide * width, 4 * count * wide * width),
    )(mine, emitted, w_key, w_value)


def exchange(block, axis, size, key):
    return lax.ppermute(block, axis, [(i, i ^ key) for i in range(size)])


def per_device(
    queries, keys_own, values_own, out_grad, summary_states, w_key, w_value, summary_grad
):
    kv_local = keys_own.shape[1] // HD
    count = summary_states.shape[0]
    n_seg = lax.axis_size("seg")
    n_tp = lax.axis_size("tp")
    position = lax.axis_index("seg").astype(jnp.int32).reshape(1)
    mine = lax.axis_index("tp").astype(jnp.int32).reshape(1)

    projected = project(summary_states, w_key, w_value)
    own = own_stats(queries, out_grad, keys_own, values_own)

    evens = sorted(range(2, n_seg, 2), key=lambda j: (j.bit_count(), -j))
    odds = [1] + [j + 1 for j in evens]
    chunks = {j: exchange(projected, "seg", n_seg, j) for j in evens}
    chunks[0] = projected
    half = n_seg // 4
    near = jnp.concatenate([chunks[j - 1] for j in odds[:half]], 0)
    far = jnp.concatenate([chunks[j - 1] for j in odds[half:]], 0)
    odd = jnp.concatenate([exchange(near, "seg", n_seg, 1), exchange(far, "seg", n_seg, 1)], 0)
    even = jnp.concatenate([chunks[j] for j in evens], 0)

    before, even_bias, odd_bias = even_stats(
        position, queries, out_grad, even, own, count, evens, odds
    )
    odd_ds, stats, odd_keys, odd_grad = slots_part(
        True, queries, out_grad, odd, before, odd_bias
    )

    got = exchange(odd_grad, "seg", n_seg, 1).astype(F32)
    even_ds, _, even_keys, even_grad = slots_part(
        False, queries, out_grad, even, stats, even_bias
    )
    blocks = {}
    for j in sorted(evens, key=lambda j: (-j.bit_length(), j)):
        at = evens.index(j) * count
        block = (even_grad[at : at + count] + got[at + count : at + 2 * count]).astype(BF16)
        blocks[j] = exchange(block, "seg", n_seg, j)
    operands = [
        queries, out_grad, keys_own, values_own, odd_keys, even_keys, odd_ds, even_ds, stats
    ]
    query_grad, *first = own_grads(0, operands, None)
    blocks, query_grad = lax.optimization_barrier((blocks, query_grad))
    emitted = got[:count]
    for block in blocks.values():
        emitted = emitted + block.astype(F32)
    emitted = emitted.astype(BF16)

    wide = w_key.shape[0] // n_tp
    terms = {}
    for group in (list(range(n_tp - 1, 1, -1)), [1, 0]):
        terms.update(zip(group, state_part(mine, emitted, w_key, w_value, wide, group)))
    bit = 1
    while bit < n_tp:
        for j in sorted((j for j in terms if j & bit), reverse=True):
            got = exchange(terms.pop(j).astype(BF16), "tp", n_tp, bit)
            terms[j ^ bit] = terms[j ^ bit].astype(F32) + got.astype(F32)
        bit *= 2
    state_grad = (terms[0] + summary_grad.astype(F32)).astype(BF16)

    key_blocks, value_blocks = [first[0]], [first[1]]
    for kv in range(1, kv_local):
        query_grad, key_block, value_block = own_grads(kv, operands, query_grad)
        key_blocks.append(key_block)
        value_blocks.append(value_block)
    key_grad = jnp.concatenate(key_blocks, 1)
    value_grad = jnp.concatenate(value_blocks, 1)
    return (query_grad, key_grad, value_grad, state_grad)


def solution(mesh):
    placed = (
        P("seg", "tp"),
        P("seg", "tp"),
        P("seg", "tp"),
        P("seg", "tp"),
        P("seg", None),
        P(None, "tp"),
        P(None, "tp"),
        P("seg", "tp"),
    )
    return jax.shard_map(
        per_device,
        mesh=mesh,
        in_specs=placed,
        out_specs=(P("seg", "tp"), P("seg", "tp"), P("seg", "tp"), P("seg", "tp")),
        check_vma=False,
    )
```

```python
import functools
import math

import jax
import jax.numpy as jnp
from jax import lax
from jax.experimental import pallas as pl
from jax.experimental.pallas import tpu as pltpu
from jax.sharding import PartitionSpec as P

HEADS = 64
KVH = 8
HD = 128
GROUP = HEADS // KVH
SCALE = HD ** (-0.5)
SCALE2 = SCALE * math.log2(math.e)
F32 = jnp.float32
BF16 = jnp.bfloat16
MIB = 1024 * 1024
LAST = (((1,), (1,)), ((), ()))
VMEM = pl.BlockSpec(memory_space=pltpu.VMEM)
ANY = pl.BlockSpec(memory_space=pl.ANY)
SMEM = pl.BlockSpec(memory_space=pltpu.SMEM)
HBM = pl.BlockSpec(memory_space=pltpu.HBM)


def dot(a, b, dims=(((1,), (0,)), ((), ()))):
    return lax.dot_general(a, b, dims, preferred_element_type=F32)


def params(mib):
    return pltpu.CompilerParams(vmem_limit_bytes=mib * MIB)


def cost(flops, nbytes):
    return pl.CostEstimate(flops=int(flops), bytes_accessed=int(nbytes), transcendentals=0)


def shape(dims, dtype=BF16):
    return jax.ShapeDtypeStruct(dims, dtype)


def lanes(index):
    return slice(index * HD, (index + 1) * HD)


def round_up(value, unit):
    return -(-value // unit) * unit


def project_kernel(
    pieces, states_hbm, wk_hbm, wv_hbm, out_ref, wk_ref, wv_ref, states_ref, sems
):
    width = wk_ref.shape[1]
    states_copy = pltpu.make_async_copy(states_hbm, states_ref, sems.at[2 * len(pieces)])
    states_copy.start()
    copies = []
    for at, (start, stop) in enumerate(pieces):
        rows = pl.ds(start, stop - start)
        pair = (
            pltpu.make_async_copy(wk_hbm.at[rows], wk_ref.at[rows], sems.at[2 * at]),
            pltpu.make_async_copy(wv_hbm.at[rows], wv_ref.at[rows], sems.at[2 * at + 1]),
        )
        for copy in pair:
            copy.start()
        copies.append(pair)
    states_copy.wait()
    keys = values = None
    for (start, stop), pair in zip(pieces, copies):
        states = states_ref[:, start:stop]
        for copy in pair:
            copy.wait()
        key_term = dot(states, wk_ref[start:stop, :])
        value_term = dot(states, wv_ref[start:stop, :])
        keys = key_term if keys is None else keys + key_term
        values = value_term if values is None else values + value_term
    out_ref[:, :width] = keys.astype(BF16)
    out_ref[:, width:] = values.astype(BF16)


def project(states, w_key, w_value):
    rows, depth = states.shape
    edges = [depth * part // 64 for part in (0, 8, 16, 24, 32, 40, 48, 56, 60, 62, 63, 64)]
    pieces = list(zip(edges, edges[1:]))
    width = w_key.shape[1]
    return pl.pallas_call(
        functools.partial(project_kernel, pieces),
        name="project",
        in_specs=[HBM] * 3,
        out_specs=VMEM,
        out_shape=shape((rows, 2 * width)),
        scratch_shapes=[
            pltpu.VMEM(w_key.shape, BF16),
            pltpu.VMEM(w_value.shape, BF16),
            pltpu.VMEM((rows, depth), BF16),
            pltpu.SemaphoreType.DMA((2 * len(pieces) + 1,)),
        ],
        compiler_params=params(12),
        cost_estimate=cost(4 * rows * depth * width, 8 * depth * width),
    )(*(pltpu.with_memory_space_constraint(x, pltpu.HBM) for x in (states, w_key, w_value)))


def causal_bias(count):
    key_pos = lax.broadcasted_iota(jnp.int32, (count, count), 0)
    row_pos = lax.broadcasted_iota(jnp.int32, (count, count), 1)
    return jnp.where(key_pos <= row_pos, 0.0, -jnp.inf).astype(F32)


def slot_bias(position, slots, count, dims):
    row = lax.broadcasted_iota(jnp.int32, dims, 0)
    bias = jnp.full(dims, -jnp.inf, F32)
    for at, slot in enumerate(slots):
        level = jnp.where((position ^ slot) < position, 0.0, -jnp.inf).astype(F32)
        bias = jnp.where((row >= at * count) & (row < (at + 1) * count), level, bias)
    return bias


def fill_padded(wide_ref, rows_ref):
    shown = rows_ref.shape[0]
    padded = wide_ref.shape[0]
    tail = shown // 8 * 8
    if padded > tail:
        wide_ref[tail:, :] = jnp.zeros((padded - tail, wide_ref.shape[1]), F32)
    wide_ref[:shown, :] = rows_ref[...].astype(F32)


def own_stats_kernel(q_ref, g_ref, k_ref, v_ref, stats_ref, bias_ref):
    bias_ref[...] = causal_bias(bias_ref.shape[0])
    for kv in range(k_ref.shape[1] // HD):
        keys = k_ref[:, lanes(kv)]
        values = v_ref[:, lanes(kv)]
        for head in range(kv * GROUP, (kv + 1) * GROUP):
            scores = dot(keys, q_ref[:, lanes(head)], LAST) * SCALE2 + bias_ref[...]
            top = jnp.max(scores, axis=0, keepdims=True)
            weights = jnp.exp2(scores - top)
            dprobs = dot(values, g_ref[:, lanes(head)], LAST)
            stats_ref[head, 0:1, :] = top
            stats_ref[head, 1:2, :] = jnp.sum(weights, axis=0, keepdims=True)
            stats_ref[head, 2:3, :] = jnp.sum(weights * dprobs, axis=0, keepdims=True)


def own_stats(queries, out_grad, keys_own, values_own):
    rows = queries.shape[0]
    heads = queries.shape[1] // HD
    return pl.pallas_call(
        own_stats_kernel,
        name="own_stats",
        in_specs=[VMEM] * 4,
        out_specs=VMEM,
        out_shape=shape((heads, 8, rows), F32),
        scratch_shapes=[pltpu.VMEM((rows, rows), F32)],
        compiler_params=params(12),
        cost_estimate=cost(20 * heads * rows * rows * HD, 4 * rows * heads * HD),
    )(queries, out_grad, keys_own, values_own)


def even_stats_kernel(
    count, evens, odds, seg_ref, q_ref, g_ref, even_ref, own_ref,
    stats_ref, even_bias_ref, odd_bias_ref, wide_ref,
):
    position = seg_ref[0]
    width = even_ref.shape[1] // 2
    even_bias_ref[...] = slot_bias(position, evens, count, even_bias_ref.shape)
    odd_bias_ref[...] = slot_bias(position, odds, count, odd_bias_ref.shape)
    fill_padded(wide_ref, even_ref)
    for kv in range(width // HD):
        keys = wide_ref[:, lanes(kv)].astype(BF16)
        values = wide_ref[:, lanes(width // HD + kv)].astype(BF16)
        for head in range(kv * GROUP, (kv + 1) * GROUP):
            scores = dot(keys, q_ref[:, lanes(head)], LAST) * SCALE2 + even_bias_ref[...]
            own_top = own_ref[head, 0:1, :]
            top = jnp.maximum(jnp.max(scores, axis=0, keepdims=True), own_top)
            weights = jnp.exp2(scores - top)
            shrink = jnp.exp2(own_top - top)
            dprobs = dot(values, g_ref[:, lanes(head)], LAST)
            total = jnp.sum(weights, axis=0, keepdims=True)
            mixed = jnp.sum(weights * dprobs, axis=0, keepdims=True)
            stats_ref[head, 0:1, :] = top
            stats_ref[head, 1:2, :] = total + own_ref[head, 1:2, :] * shrink
            stats_ref[head, 2:3, :] = mixed + own_ref[head, 2:3, :] * shrink


def even_stats(position, queries, out_grad, even, own, count, evens, odds):
    rows = queries.shape[0]
    heads = queries.shape[1] // HD
    padded = round_up(even.shape[0], 16)
    return pl.pallas_call(
        functools.partial(even_stats_kernel, count, evens, odds),
        name="even_stats",
        in_specs=[SMEM] + [VMEM] * 4,
        out_specs=[VMEM] * 3,
        out_shape=[
            shape((heads, 8, rows), F32),
            shape((padded, rows), F32),
            shape((round_up(len(odds) * count, 16), rows), F32),
        ],
        scratch_shapes=[pltpu.VMEM((padded, even.shape[1]), F32)],
        compiler_params=params(12 if padded <= 512 else 32),
        cost_estimate=cost(20 * heads * rows * padded * HD, 4 * rows * heads * HD),
    )(position, queries, out_grad, even, own)


def slots_kernel(
    last, q_ref, g_ref, slots_ref, before_ref, bias_ref,
    ds_ref, stats_ref, keys_ref, grad_ref, wide_ref,
):
    shown = slots_ref.shape[0]
    kv_local = keys_ref.shape[1] // HD
    width = kv_local * HD
    fill_padded(wide_ref, slots_ref)
    keys_ref[...] = wide_ref[:, :width].astype(BF16)
    for kv in range(kv_local):
        keys = keys_ref[:, lanes(kv)]
        values = wide_ref[:, lanes(kv_local + kv)].astype(BF16)
        heads = range(kv * GROUP, (kv + 1) * GROUP)
        all_dscores, all_probs = [], []
        for head in heads:
            scores = dot(keys, q_ref[:, lanes(head)], LAST) * SCALE2 + bias_ref[...]
            dprobs = dot(values, g_ref[:, lanes(head)], LAST)
            old_top = before_ref[head, 0:1, :]
            if last:
                top = jnp.maximum(jnp.max(scores, axis=0, keepdims=True), old_top)
                weights = jnp.exp2(scores - top)
                shrink = jnp.exp2(old_top - top)
                total = jnp.sum(weights, axis=0, keepdims=True)
                inverse = 1.0 / (total + before_ref[head, 1:2, :] * shrink)
                mixed = jnp.sum(weights * dprobs, axis=0, keepdims=True)
                delta = (mixed + before_ref[head, 2:3, :] * shrink) * inverse
                probs = weights * inverse
                stats_ref[head, 0:1, :] = top
                stats_ref[head, 1:2, :] = inverse
                stats_ref[head, 2:3, :] = delta
            else:
                probs = jnp.exp2(scores - old_top) * before_ref[head, 1:2, :]
                delta = before_ref[head, 2:3, :]
            dscores = (probs * (dprobs - delta)).astype(BF16)
            ds_ref[head] = dscores
            all_dscores.append(dscores)
            all_probs.append(probs.astype(BF16))
        queries = jnp.concatenate([q_ref[:, lanes(head)] for head in heads], 0)
        grads = jnp.concatenate([g_ref[:, lanes(head)] for head in heads], 0)
        key_part = dot(jnp.concatenate(all_dscores, 1), queries) * SCALE
        value_part = dot(jnp.concatenate(all_probs, 1), grads)
        grad_ref[:, lanes(kv)] = key_part[:shown].astype(grad_ref.dtype)
        grad_ref[:, lanes(kv_local + kv)] = value_part[:shown].astype(grad_ref.dtype)
    if not last:
        stats_ref[...] = jnp.zeros_like(stats_ref)


def slots_part(last, queries, out_grad, slots, before, bias):
    rows = queries.shape[0]
    shown, width = slots.shape[0], slots.shape[1] // 2
    heads = queries.shape[1] // HD
    padded = round_up(shown, 16)
    return pl.pallas_call(
        functools.partial(slots_kernel, last),
        name="odd_slots" if last else "even_slots",
        in_specs=[VMEM] * 5,
        out_specs=[VMEM] * 4,
        out_shape=[
            shape((heads, padded, rows)),
            shape((heads, 8, rows) if last else (8, HD), F32),
            shape((padded, width)),
            shape(slots.shape, BF16 if last else F32),
        ],
        scratch_shapes=[pltpu.VMEM((padded, 2 * width), F32)],
        compiler_params=params(16 if padded <= 512 else 40),
        cost_estimate=cost(30 * heads * rows * padded * HD, 4 * rows * heads * HD),
    )(queries, out_grad, slots, before, bias)


def own_grads_kernel(
    kv, q_ref, g_ref, k_ref, v_ref, ok_ref, ek_ref, ods_ref, eds_ref, stats_ref, *rest
):
    dq_out, dk_ref, dv_ref, bias_ref, dq_ref, sem = rest[-6:]
    bias_ref[...] = causal_bias(bias_ref.shape[0])
    keys = k_ref[:, lanes(kv)]
    values = v_ref[:, lanes(kv)]
    keys_t = jnp.concatenate([ok_ref[:, lanes(kv)], ek_ref[:, lanes(kv)], keys], 0).T
    heads = range(kv * GROUP, (kv + 1) * GROUP)
    all_dscores, all_probs = [], []
    for at, head in enumerate(heads):
        scores = dot(keys, q_ref[:, lanes(head)], LAST) * SCALE2 + bias_ref[...]
        probs = jnp.exp2(scores - stats_ref[head, 0:1, :]) * stats_ref[head, 1:2, :]
        dprobs = dot(values, g_ref[:, lanes(head)], LAST)
        dscores = (probs * (dprobs - stats_ref[head, 2:3, :])).astype(BF16)
        all_dscores.append(dscores)
        all_probs.append(probs.astype(BF16))
        dquery = dot(keys_t, jnp.concatenate([ods_ref[head], eds_ref[head], dscores], 0))
        dq_ref[:, lanes(at)] = (dquery * SCALE).T.astype(BF16)
    columns = pl.ds(kv * GROUP * HD, GROUP * HD)
    copy = pltpu.make_async_copy(dq_ref, dq_out.at[:, columns], sem)
    copy.start()
    queries = jnp.concatenate([q_ref[:, lanes(head)] for head in heads], 0)
    grads = jnp.concatenate([g_ref[:, lanes(head)] for head in heads], 0)
    dk_ref[...] = (dot(jnp.concatenate(all_dscores, 1), queries) * SCALE).astype(BF16)
    dv_ref[...] = dot(jnp.concatenate(all_probs, 1), grads).astype(BF16)
    copy.wait()


def own_grads(kv, operands, earlier):
    queries, odd_keys, even_keys = operands[0], operands[4], operands[5]
    rows = queries.shape[0]
    heads = queries.shape[1] // HD
    padded = odd_keys.shape[0] + even_keys.shape[0]
    in_specs = [VMEM] * len(operands)
    aliases = {}
    if earlier is not None:
        aliases = {len(operands): 0}
        operands = [*operands, earlier]
        in_specs.append(HBM)
    return pl.pallas_call(
        functools.partial(own_grads_kernel, kv),
        name="own_grads",
        in_specs=in_specs,
        out_specs=[HBM, VMEM, VMEM],
        out_shape=[shape((rows, heads * HD)), shape((rows, HD)), shape((rows, HD))],
        input_output_aliases=aliases,
        scratch_shapes=[
            pltpu.VMEM((rows, rows), F32),
            pltpu.VMEM((rows, GROUP * HD), BF16),
            pltpu.SemaphoreType.DMA,
        ],
        compiler_params=params(16 if padded <= 512 else 32),
        cost_estimate=cost(20 * heads * rows * rows * HD, 4 * rows * heads * HD),
    )(*operands)


def state_kernel(chunk, group, mine_ref, emitted_ref, wk_ref, wv_ref, *out_refs):
    width = wk_ref.shape[1]
    keys = emitted_ref[:, :width]
    values = emitted_ref[:, width:]
    wide = out_refs[0].shape[1]
    for at, out_ref in enumerate(out_refs):
        for step in range(wide // chunk):
            rows = pl.ds(pl.multiple_of((mine_ref[0] ^ group[at]) * wide + step * chunk, chunk), chunk)
            total = dot(keys, wk_ref[rows, :], LAST) + dot(values, wv_ref[rows, :], LAST)
            out_ref[:, step * chunk : (step + 1) * chunk] = total.astype(BF16)


def state_part(mine, emitted, w_key, w_value, wide, group, chunk=512):
    rows = emitted.shape[0]
    width = w_key.shape[1]
    count = len(group)
    return pl.pallas_call(
        functools.partial(state_kernel, chunk, group),
        name="state_part",
        in_specs=[SMEM] + [VMEM] * 3,
        out_specs=[VMEM] * count,
        out_shape=[shape((rows, wide))] * count,
        compiler_params=params(14),
        cost_estimate=cost(4 * rows * count * wide * width, 4 * count * wide * width),
    )(mine, emitted, w_key, w_value)


def exchange(block, axis, size, key):
    return lax.ppermute(block, axis, [(i, i ^ key) for i in range(size)])


def per_device(
    queries, keys_own, values_own, out_grad, summary_states, w_key, w_value, summary_grad
):
    kv_local = keys_own.shape[1] // HD
    count = summary_states.shape[0]
    n_seg = lax.axis_size("seg")
    n_tp = lax.axis_size("tp")
    position = lax.axis_index("seg").astype(jnp.int32).reshape(1)
    mine = lax.axis_index("tp").astype(jnp.int32).reshape(1)

    projected = project(summary_states, w_key, w_value)
    own = own_stats(queries, out_grad, keys_own, values_own)

    near = [j for j in range(0, n_seg, 2) if not j & 2]
    far = [j for j in range(0, n_seg, 2) if j & 2]
    evens = (near + far)[1:]
    odds = [j + 1 for j in near + far]
    chunks = {j: exchange(projected, "seg", n_seg, j) for j in range(2, n_seg, 2)}
    chunks[0] = projected
    odd = jnp.concatenate(
        [
            exchange(jnp.concatenate([chunks[j] for j in group], 0), "seg", n_seg, 1)
            for group in (near, far)
        ],
        0,
    )
    even = jnp.concatenate([chunks[j] for j in evens], 0)

    before, even_bias, odd_bias = even_stats(
        position, queries, out_grad, even, own, count, evens, odds
    )
    odd_ds, stats, odd_keys, odd_grad = slots_part(
        True, queries, out_grad, odd, before, odd_bias
    )

    got = exchange(odd_grad, "seg", n_seg, 1).astype(F32)
    even_ds, _, even_keys, even_grad = slots_part(
        False, queries, out_grad, even, stats, even_bias
    )
    blocks = {}
    for j in sorted(evens, key=lambda j: (j.bit_count(), -j)):
        at = evens.index(j) * count
        block = (even_grad[at : at + count] + got[at + count : at + 2 * count]).astype(BF16)
        blocks[j] = exchange(block, "seg", n_seg, j)
    operands = [
        queries, out_grad, keys_own, values_own, odd_keys, even_keys, odd_ds, even_ds, stats
    ]
    query_grad, *first = own_grads(0, operands, None)
    blocks, query_grad = lax.optimization_barrier((blocks, query_grad))
    emitted = got[:count]
    for block in blocks.values():
        emitted = emitted + block.astype(F32)
    emitted = emitted.astype(BF16)

    wide = w_key.shape[0] // n_tp
    far_group, near_group = list(range(n_tp - 1, 1, -1)), [1, 0]
    terms = {}
    for group in ([j for j in far_group if j & 1], [j for j in far_group if not j & 1]):
        terms.update(zip(group, state_part(mine, emitted, w_key, w_value, wide, group)))
    bit = 1
    while bit < n_tp:
        for j in sorted((j for j in terms if j & bit and j > bit), reverse=True):
            got = exchange(terms.pop(j).astype(BF16), "tp", n_tp, bit)
            terms[j ^ bit] = terms[j ^ bit].astype(F32) + got.astype(F32)
        bit *= 2
    terms = {j: terms[j].astype(BF16) for j in terms}
    terms, emitted = lax.optimization_barrier((terms, emitted))
    sent = {j: exchange(terms[j], "tp", n_tp, j) for j in terms}
    other, state = state_part(mine, emitted, w_key, w_value, wide, near_group)
    state = state.astype(F32) + exchange(other, "tp", n_tp, 1).astype(F32)
    for j in sent:
        state = state + sent[j].astype(F32)
    terms = {0: state}
    state_grad = (terms[0] + summary_grad.astype(F32)).astype(BF16)

    key_blocks, value_blocks = [first[0]], [first[1]]
    for kv in range(1, kv_local):
        query_grad, key_block, value_block = own_grads(kv, operands, query_grad)
        key_blocks.append(key_block)
        value_blocks.append(value_block)
    key_grad = jnp.concatenate(key_blocks, 1)
    value_grad = jnp.concatenate(value_blocks, 1)
    return (query_grad, key_grad, value_grad, state_grad)


def solution(mesh):
    placed = (
        P("seg", "tp"),
        P("seg", "tp"),
        P("seg", "tp"),
        P("seg", "tp"),
        P("seg", None),
        P(None, "tp"),
        P(None, "tp"),
        P("seg", "tp"),
    )
    return jax.shard_map(
        per_device,
        mesh=mesh,
        in_specs=placed,
        out_specs=(P("seg", "tp"), P("seg", "tp"), P("seg", "tp"), P("seg", "tp")),
        check_vma=False,
    )
```

```python
import functools
import math

import jax
import jax.numpy as jnp
from jax import lax
from jax.experimental import pallas as pl
from jax.experimental.pallas import tpu as pltpu
from jax.sharding import PartitionSpec as P

HEADS = 64
KVH = 8
HD = 128
GROUP = HEADS // KVH
SCALE = HD ** (-0.5)
SCALE2 = SCALE * math.log2(math.e)
F32 = jnp.float32
BF16 = jnp.bfloat16
MIB = 1024 * 1024
LAST = (((1,), (1,)), ((), ()))
VMEM = pl.BlockSpec(memory_space=pltpu.VMEM)
ANY = pl.BlockSpec(memory_space=pl.ANY)
SMEM = pl.BlockSpec(memory_space=pltpu.SMEM)
HBM = pl.BlockSpec(memory_space=pltpu.HBM)


def dot(a, b, dims=(((1,), (0,)), ((), ()))):
    return lax.dot_general(a, b, dims, preferred_element_type=F32)


def params(mib):
    return pltpu.CompilerParams(vmem_limit_bytes=mib * MIB)


def cost(flops, nbytes):
    return pl.CostEstimate(flops=int(flops), bytes_accessed=int(nbytes), transcendentals=0)


def shape(dims, dtype=BF16):
    return jax.ShapeDtypeStruct(dims, dtype)


def lanes(index):
    return slice(index * HD, (index + 1) * HD)


def round_up(value, unit):
    return -(-value // unit) * unit


def project_kernel(
    pieces, states_hbm, wk_hbm, wv_hbm, out_ref, wk_ref, wv_ref, states_ref, sems
):
    width = wk_ref.shape[1]
    states_copy = pltpu.make_async_copy(states_hbm, states_ref, sems.at[2 * len(pieces)])
    states_copy.start()
    copies = []
    for at, (start, stop) in enumerate(pieces):
        rows = pl.ds(start, stop - start)
        pair = (
            pltpu.make_async_copy(wk_hbm.at[rows], wk_ref.at[rows], sems.at[2 * at]),
            pltpu.make_async_copy(wv_hbm.at[rows], wv_ref.at[rows], sems.at[2 * at + 1]),
        )
        for copy in pair:
            copy.start()
        copies.append(pair)
    states_copy.wait()
    keys = values = None
    for (start, stop), pair in zip(pieces, copies):
        states = states_ref[:, start:stop]
        for copy in pair:
            copy.wait()
        key_term = dot(states, wk_ref[start:stop, :])
        value_term = dot(states, wv_ref[start:stop, :])
        keys = key_term if keys is None else keys + key_term
        values = value_term if values is None else values + value_term
    out_ref[:, :width] = keys.astype(BF16)
    out_ref[:, width:] = values.astype(BF16)


def project(states, w_key, w_value):
    rows, depth = states.shape
    edges = [depth * part // 64 for part in (0, 8, 16, 24, 32, 40, 48, 56, 60, 62, 63, 64)]
    pieces = list(zip(edges, edges[1:]))
    width = w_key.shape[1]
    return pl.pallas_call(
        functools.partial(project_kernel, pieces),
        name="project",
        in_specs=[HBM] * 3,
        out_specs=VMEM,
        out_shape=shape((rows, 2 * width)),
        scratch_shapes=[
            pltpu.VMEM(w_key.shape, BF16),
            pltpu.VMEM(w_value.shape, BF16),
            pltpu.VMEM((rows, depth), BF16),
            pltpu.SemaphoreType.DMA((2 * len(pieces) + 1,)),
        ],
        compiler_params=params(12),
        cost_estimate=cost(4 * rows * depth * width, 8 * depth * width),
    )(*(pltpu.with_memory_space_constraint(x, pltpu.HBM) for x in (states, w_key, w_value)))


def causal_bias(count):
    key_pos = lax.broadcasted_iota(jnp.int32, (count, count), 0)
    row_pos = lax.broadcasted_iota(jnp.int32, (count, count), 1)
    return jnp.where(key_pos <= row_pos, 0.0, -jnp.inf).astype(F32)


def slot_bias(position, slots, count, dims):
    row = lax.broadcasted_iota(jnp.int32, dims, 0)
    bias = jnp.full(dims, -jnp.inf, F32)
    for at, slot in enumerate(slots):
        level = jnp.where((position ^ slot) < position, 0.0, -jnp.inf).astype(F32)
        bias = jnp.where((row >= at * count) & (row < (at + 1) * count), level, bias)
    return bias


def fill_padded(wide_ref, rows_ref):
    shown = rows_ref.shape[0]
    padded = wide_ref.shape[0]
    tail = shown // 8 * 8
    if padded > tail:
        wide_ref[tail:, :] = jnp.zeros((padded - tail, wide_ref.shape[1]), F32)
    wide_ref[:shown, :] = rows_ref[...].astype(F32)


def own_stats_kernel(q_ref, g_ref, k_ref, v_ref, stats_ref, bias_ref):
    bias_ref[...] = causal_bias(bias_ref.shape[0])
    for kv in range(k_ref.shape[1] // HD):
        keys = k_ref[:, lanes(kv)]
        values = v_ref[:, lanes(kv)]
        for head in range(kv * GROUP, (kv + 1) * GROUP):
            scores = dot(keys, q_ref[:, lanes(head)], LAST) * SCALE2 + bias_ref[...]
            top = jnp.max(scores, axis=0, keepdims=True)
            weights = jnp.exp2(scores - top)
            dprobs = dot(values, g_ref[:, lanes(head)], LAST)
            stats_ref[head, 0:1, :] = top
            stats_ref[head, 1:2, :] = jnp.sum(weights, axis=0, keepdims=True)
            stats_ref[head, 2:3, :] = jnp.sum(weights * dprobs, axis=0, keepdims=True)


def own_stats(queries, out_grad, keys_own, values_own):
    rows = queries.shape[0]
    heads = queries.shape[1] // HD
    return pl.pallas_call(
        own_stats_kernel,
        name="own_stats",
        in_specs=[VMEM] * 4,
        out_specs=VMEM,
        out_shape=shape((heads, 8, rows), F32),
        scratch_shapes=[pltpu.VMEM((rows, rows), F32)],
        compiler_params=params(12),
        cost_estimate=cost(20 * heads * rows * rows * HD, 4 * rows * heads * HD),
    )(queries, out_grad, keys_own, values_own)


def even_stats_kernel(
    count, evens, odds, seg_ref, q_ref, g_ref, even_ref, own_ref,
    stats_ref, even_bias_ref, odd_bias_ref, wide_ref,
):
    position = seg_ref[0]
    width = even_ref.shape[1] // 2
    even_bias_ref[...] = slot_bias(position, evens, count, even_bias_ref.shape)
    odd_bias_ref[...] = slot_bias(position, odds, count, odd_bias_ref.shape)
    fill_padded(wide_ref, even_ref)
    for kv in range(width // HD):
        keys = wide_ref[:, lanes(kv)].astype(BF16)
        values = wide_ref[:, lanes(width // HD + kv)].astype(BF16)
        for head in range(kv * GROUP, (kv + 1) * GROUP):
            scores = dot(keys, q_ref[:, lanes(head)], LAST) * SCALE2 + even_bias_ref[...]
            own_top = own_ref[head, 0:1, :]
            top = jnp.maximum(jnp.max(scores, axis=0, keepdims=True), own_top)
            weights = jnp.exp2(scores - top)
            shrink = jnp.exp2(own_top - top)
            dprobs = dot(values, g_ref[:, lanes(head)], LAST)
            total = jnp.sum(weights, axis=0, keepdims=True)
            mixed = jnp.sum(weights * dprobs, axis=0, keepdims=True)
            stats_ref[head, 0:1, :] = top
            stats_ref[head, 1:2, :] = total + own_ref[head, 1:2, :] * shrink
            stats_ref[head, 2:3, :] = mixed + own_ref[head, 2:3, :] * shrink


def even_stats(position, queries, out_grad, even, own, count, evens, odds):
    rows = queries.shape[0]
    heads = queries.shape[1] // HD
    padded = round_up(even.shape[0], 16)
    return pl.pallas_call(
        functools.partial(even_stats_kernel, count, evens, odds),
        name="even_stats",
        in_specs=[SMEM] + [VMEM] * 4,
        out_specs=[VMEM] * 3,
        out_shape=[
            shape((heads, 8, rows), F32),
            shape((padded, rows), F32),
            shape((round_up(len(odds) * count, 16), rows), F32),
        ],
        scratch_shapes=[pltpu.VMEM((padded, even.shape[1]), F32)],
        compiler_params=params(12 if padded <= 512 else 32),
        cost_estimate=cost(20 * heads * rows * padded * HD, 4 * rows * heads * HD),
    )(position, queries, out_grad, even, own)


def slots_kernel(
    last, q_ref, g_ref, slots_ref, before_ref, bias_ref,
    ds_ref, stats_ref, keys_ref, grad_ref, wide_ref,
):
    shown = slots_ref.shape[0]
    kv_local = keys_ref.shape[1] // HD
    width = kv_local * HD
    fill_padded(wide_ref, slots_ref)
    keys_ref[...] = wide_ref[:, :width].astype(BF16)
    for kv in range(kv_local):
        keys = keys_ref[:, lanes(kv)]
        values = wide_ref[:, lanes(kv_local + kv)].astype(BF16)
        heads = range(kv * GROUP, (kv + 1) * GROUP)
        all_dscores, all_probs = [], []
        for head in heads:
            scores = dot(keys, q_ref[:, lanes(head)], LAST) * SCALE2 + bias_ref[...]
            dprobs = dot(values, g_ref[:, lanes(head)], LAST)
            old_top = before_ref[head, 0:1, :]
            if last:
                top = jnp.maximum(jnp.max(scores, axis=0, keepdims=True), old_top)
                weights = jnp.exp2(scores - top)
                shrink = jnp.exp2(old_top - top)
                total = jnp.sum(weights, axis=0, keepdims=True)
                inverse = 1.0 / (total + before_ref[head, 1:2, :] * shrink)
                mixed = jnp.sum(weights * dprobs, axis=0, keepdims=True)
                delta = (mixed + before_ref[head, 2:3, :] * shrink) * inverse
                probs = weights * inverse
                stats_ref[head, 0:1, :] = top
                stats_ref[head, 1:2, :] = inverse
                stats_ref[head, 2:3, :] = delta
            else:
                probs = jnp.exp2(scores - old_top) * before_ref[head, 1:2, :]
                delta = before_ref[head, 2:3, :]
            dscores = (probs * (dprobs - delta)).astype(BF16)
            ds_ref[head] = dscores
            all_dscores.append(dscores)
            all_probs.append(probs.astype(BF16))
        queries = jnp.concatenate([q_ref[:, lanes(head)] for head in heads], 0)
        grads = jnp.concatenate([g_ref[:, lanes(head)] for head in heads], 0)
        key_part = dot(jnp.concatenate(all_dscores, 1), queries) * SCALE
        value_part = dot(jnp.concatenate(all_probs, 1), grads)
        grad_ref[:, lanes(kv)] = key_part[:shown].astype(grad_ref.dtype)
        grad_ref[:, lanes(kv_local + kv)] = value_part[:shown].astype(grad_ref.dtype)
    if not last:
        stats_ref[...] = jnp.zeros_like(stats_ref)


def slots_part(last, queries, out_grad, slots, before, bias):
    rows = queries.shape[0]
    shown, width = slots.shape[0], slots.shape[1] // 2
    heads = queries.shape[1] // HD
    padded = round_up(shown, 16)
    return pl.pallas_call(
        functools.partial(slots_kernel, last),
        name="odd_slots" if last else "even_slots",
        in_specs=[VMEM] * 5,
        out_specs=[VMEM] * 4,
        out_shape=[
            shape((heads, padded, rows)),
            shape((heads, 8, rows) if last else (8, HD), F32),
            shape((padded, width)),
            shape(slots.shape, BF16 if last else F32),
        ],
        scratch_shapes=[pltpu.VMEM((padded, 2 * width), F32)],
        compiler_params=params(16 if padded <= 512 else 40),
        cost_estimate=cost(30 * heads * rows * padded * HD, 4 * rows * heads * HD),
    )(queries, out_grad, slots, before, bias)


def own_grads_kernel(
    heads, last, q_ref, g_ref, k_ref, v_ref, ok_ref, ek_ref, ods_ref, eds_ref, stats_ref, *rest
):
    *earlier, dq_out, dk_ref, dv_ref, bias_ref, dq_ref, sem = rest
    kv = heads[0] // GROUP
    bias_ref[...] = causal_bias(bias_ref.shape[0])
    keys = k_ref[:, lanes(kv)]
    values = v_ref[:, lanes(kv)]
    keys_t = jnp.concatenate([ok_ref[:, lanes(kv)], ek_ref[:, lanes(kv)], keys], 0).T
    all_dscores, all_probs = [], []
    for at, head in enumerate(heads):
        scores = dot(keys, q_ref[:, lanes(head)], LAST) * SCALE2 + bias_ref[...]
        probs = jnp.exp2(scores - stats_ref[head, 0:1, :]) * stats_ref[head, 1:2, :]
        dprobs = dot(values, g_ref[:, lanes(head)], LAST)
        dscores = (probs * (dprobs - stats_ref[head, 2:3, :])).astype(BF16)
        all_dscores.append(dscores)
        all_probs.append(probs.astype(BF16))
        dquery = dot(keys_t, jnp.concatenate([ods_ref[head], eds_ref[head], dscores], 0))
        dq_ref[:, lanes(at)] = (dquery * SCALE).T.astype(BF16)
    columns = pl.ds(heads[0] * HD, len(heads) * HD)
    copy = pltpu.make_async_copy(dq_ref, dq_out.at[:, columns], sem)
    copy.start()
    queries = jnp.concatenate([q_ref[:, lanes(head)] for head in heads], 0)
    grads = jnp.concatenate([g_ref[:, lanes(head)] for head in heads], 0)
    key_part = dot(jnp.concatenate(all_dscores, 1), queries)
    value_part = dot(jnp.concatenate(all_probs, 1), grads)
    if len(earlier) > 1:
        key_part = key_part + earlier[1][...]
        value_part = value_part + earlier[2][...]
    if last:
        key_part = key_part * SCALE
    dk_ref[...] = key_part.astype(dk_ref.dtype)
    dv_ref[...] = value_part.astype(dv_ref.dtype)
    copy.wait()


def own_grads(heads, last, operands, earlier):
    queries, odd_keys, even_keys = operands[0], operands[4], operands[5]
    rows = queries.shape[0]
    padded = odd_keys.shape[0] + even_keys.shape[0]
    in_specs = [VMEM] * len(operands) + [HBM, VMEM, VMEM][: len(earlier)]
    aliases = {len(operands): 0} if earlier else {}
    kind = BF16 if last else F32
    return pl.pallas_call(
        functools.partial(own_grads_kernel, heads, last),
        name="own_grads",
        in_specs=in_specs,
        out_specs=[HBM, VMEM, VMEM],
        out_shape=[shape(queries.shape), shape((rows, HD), kind), shape((rows, HD), kind)],
        input_output_aliases=aliases,
        scratch_shapes=[
            pltpu.VMEM((rows, rows), F32),
            pltpu.VMEM((rows, len(heads) * HD), BF16),
            pltpu.SemaphoreType.DMA,
        ],
        compiler_params=params(16 if padded <= 512 else 32),
        cost_estimate=cost(20 * len(heads) * rows * rows * HD, 4 * rows * len(heads) * HD),
    )(*operands, *earlier)


def state_kernel(chunk, group, mine_ref, emitted_ref, wk_ref, wv_ref, *out_refs):
    width = wk_ref.shape[1]
    keys = emitted_ref[:, :width]
    values = emitted_ref[:, width:]
    wide = out_refs[0].shape[1]
    for at, out_ref in enumerate(out_refs):
        for step in range(wide // chunk):
            rows = pl.ds(pl.multiple_of((mine_ref[0] ^ group[at]) * wide + step * chunk, chunk), chunk)
            total = dot(keys, wk_ref[rows, :], LAST) + dot(values, wv_ref[rows, :], LAST)
            out_ref[:, step * chunk : (step + 1) * chunk] = total.astype(BF16)


def state_part(mine, emitted, w_key, w_value, wide, group, chunk=512):
    rows = emitted.shape[0]
    width = w_key.shape[1]
    count = len(group)
    return pl.pallas_call(
        functools.partial(state_kernel, chunk, group),
        name="state_part",
        in_specs=[SMEM] + [VMEM] * 3,
        out_specs=[VMEM] * count,
        out_shape=[shape((rows, wide))] * count,
        compiler_params=params(14),
        cost_estimate=cost(4 * rows * count * wide * width, 4 * count * wide * width),
    )(mine, emitted, w_key, w_value)


def exchange(block, axis, size, key):
    return lax.ppermute(block, axis, [(i, i ^ key) for i in range(size)])


def per_device(
    queries, keys_own, values_own, out_grad, summary_states, w_key, w_value, summary_grad
):
    kv_local = keys_own.shape[1] // HD
    count = summary_states.shape[0]
    n_seg = lax.axis_size("seg")
    n_tp = lax.axis_size("tp")
    position = lax.axis_index("seg").astype(jnp.int32).reshape(1)
    mine = lax.axis_index("tp").astype(jnp.int32).reshape(1)

    projected = project(summary_states, w_key, w_value)
    own = own_stats(queries, out_grad, keys_own, values_own)

    near = [j for j in range(0, n_seg, 2) if not j & 2]
    far = [j for j in range(0, n_seg, 2) if j & 2]
    evens = (near + far)[1:]
    odds = [j + 1 for j in near + far]
    chunks = {j: exchange(projected, "seg", n_seg, j) for j in range(2, n_seg, 2)}
    chunks[0] = projected
    odd = jnp.concatenate(
        [
            exchange(jnp.concatenate([chunks[j] for j in group], 0), "seg", n_seg, 1)
            for group in (near, far)
        ],
        0,
    )
    even = jnp.concatenate([chunks[j] for j in evens], 0)

    before, even_bias, odd_bias = even_stats(
        position, queries, out_grad, even, own, count, evens, odds
    )
    odd_ds, stats, odd_keys, odd_grad = slots_part(
        True, queries, out_grad, odd, before, odd_bias
    )

    got = exchange(odd_grad, "seg", n_seg, 1)
    even_ds, _, even_keys, even_grad = slots_part(
        False, queries, out_grad, even, stats, even_bias
    )
    operands = [
        queries, out_grad, keys_own, values_own, odd_keys, even_keys, odd_ds, even_ds, stats
    ]
    begun = own_grads(range(GROUP // 2), False, operands, [])
    got, even_grad, begun = lax.optimization_barrier((got, even_grad, begun))
    blocks = {}
    for j in sorted(evens, key=lambda j: (j.bit_count(), -j)):
        at = evens.index(j) * count
        block = got[at + count : at + 2 * count].astype(F32) + even_grad[at : at + count]
        block = block.astype(BF16)
        blocks[j] = exchange(block, "seg", n_seg, j)
    query_grad, *first = own_grads(range(GROUP // 2, GROUP), True, operands, begun)
    blocks, query_grad = lax.optimization_barrier((blocks, query_grad))
    emitted = got[:count].astype(F32)
    for block in blocks.values():
        emitted = emitted + block.astype(F32)
    emitted = emitted.astype(BF16)

    wide = w_key.shape[0] // n_tp
    far_group, near_group = list(range(n_tp - 1, 1, -1)), [1, 0]
    terms = {}
    for group in ([j for j in far_group if j & 1], [j for j in far_group if not j & 1]):
        terms.update(zip(group, state_part(mine, emitted, w_key, w_value, wide, group)))
    bit = 1
    while bit < n_tp:
        for j in sorted((j for j in terms if j & bit and j > bit), reverse=True):
            got = exchange(terms.pop(j).astype(BF16), "tp", n_tp, bit)
            terms[j ^ bit] = terms[j ^ bit].astype(F32) + got.astype(F32)
        bit *= 2
    terms = {j: terms[j].astype(BF16) for j in terms}
    terms, emitted = lax.optimization_barrier((terms, emitted))
    sent = {j: exchange(terms[j], "tp", n_tp, j) for j in terms}
    other, state = state_part(mine, emitted, w_key, w_value, wide, near_group)
    state = state.astype(F32) + exchange(other, "tp", n_tp, 1).astype(F32)
    for j in sent:
        state = state + sent[j].astype(F32)
    terms = {0: state}
    state_grad = (terms[0] + summary_grad.astype(F32)).astype(BF16)

    key_blocks, value_blocks = [first[0]], [first[1]]
    for kv in range(1, kv_local):
        query_grad, key_block, value_block = own_grads(
            range(kv * GROUP, (kv + 1) * GROUP), True, operands, [query_grad]
        )
        key_blocks.append(key_block)
        value_blocks.append(value_block)
    key_grad = jnp.concatenate(key_blocks, 1)
    value_grad = jnp.concatenate(value_blocks, 1)
    return (query_grad, key_grad, value_grad, state_grad)


def solution(mesh):
    placed = (
        P("seg", "tp"),
        P("seg", "tp"),
        P("seg", "tp"),
        P("seg", "tp"),
        P("seg", None),
        P(None, "tp"),
        P(None, "tp"),
        P("seg", "tp"),
    )
    return jax.shard_map(
        per_device,
        mesh=mesh,
        in_specs=placed,
        out_specs=(P("seg", "tp"), P("seg", "tp"), P("seg", "tp"), P("seg", "tp")),
        check_vma=False,
    )
```

```python
import functools
import math

import jax
import jax.numpy as jnp
from jax import lax
from jax.experimental import pallas as pl
from jax.experimental.pallas import tpu as pltpu
from jax.sharding import PartitionSpec as P

HEADS = 64
KVH = 8
HD = 128
GROUP = HEADS // KVH
SCALE = HD ** (-0.5)
SCALE2 = SCALE * math.log2(math.e)
F32 = jnp.float32
BF16 = jnp.bfloat16
MIB = 1024 * 1024
LAST = (((1,), (1,)), ((), ()))
VMEM = pl.BlockSpec(memory_space=pltpu.VMEM)
ANY = pl.BlockSpec(memory_space=pl.ANY)
SMEM = pl.BlockSpec(memory_space=pltpu.SMEM)
HBM = pl.BlockSpec(memory_space=pltpu.HBM)


def dot(a, b, dims=(((1,), (0,)), ((), ()))):
    return lax.dot_general(a, b, dims, preferred_element_type=F32)


def params(mib):
    return pltpu.CompilerParams(vmem_limit_bytes=mib * MIB)


def cost(flops, nbytes):
    return pl.CostEstimate(flops=int(flops), bytes_accessed=int(nbytes), transcendentals=0)


def shape(dims, dtype=BF16):
    return jax.ShapeDtypeStruct(dims, dtype)


def lanes(index):
    return slice(index * HD, (index + 1) * HD)


def round_up(value, unit):
    return -(-value // unit) * unit


def project_kernel(
    pieces, states_hbm, wk_hbm, wv_hbm, out_ref, wk_ref, wv_ref, states_ref, sems
):
    width = wk_ref.shape[1]
    states_copy = pltpu.make_async_copy(states_hbm, states_ref, sems.at[2 * len(pieces)])
    states_copy.start()
    copies = []
    for at, (start, stop) in enumerate(pieces):
        rows = pl.ds(start, stop - start)
        pair = (
            pltpu.make_async_copy(wk_hbm.at[rows], wk_ref.at[rows], sems.at[2 * at]),
            pltpu.make_async_copy(wv_hbm.at[rows], wv_ref.at[rows], sems.at[2 * at + 1]),
        )
        for copy in pair:
            copy.start()
        copies.append(pair)
    states_copy.wait()
    keys = values = None
    for (start, stop), pair in zip(pieces, copies):
        states = states_ref[:, start:stop]
        for copy in pair:
            copy.wait()
        key_term = dot(states, wk_ref[start:stop, :])
        value_term = dot(states, wv_ref[start:stop, :])
        keys = key_term if keys is None else keys + key_term
        values = value_term if values is None else values + value_term
    out_ref[:, :width] = keys.astype(BF16)
    out_ref[:, width:] = values.astype(BF16)


def project(states, w_key, w_value):
    rows, depth = states.shape
    edges = [depth * part // 64 for part in (0, 8, 16, 24, 32, 40, 48, 56, 60, 62, 63, 64)]
    pieces = list(zip(edges, edges[1:]))
    width = w_key.shape[1]
    return pl.pallas_call(
        functools.partial(project_kernel, pieces),
        name="project",
        in_specs=[HBM] * 3,
        out_specs=VMEM,
        out_shape=shape((rows, 2 * width)),
        scratch_shapes=[
            pltpu.VMEM(w_key.shape, BF16),
            pltpu.VMEM(w_value.shape, BF16),
            pltpu.VMEM((rows, depth), BF16),
            pltpu.SemaphoreType.DMA((2 * len(pieces) + 1,)),
        ],
        compiler_params=params(12),
        cost_estimate=cost(4 * rows * depth * width, 8 * depth * width),
    )(*(pltpu.with_memory_space_constraint(x, pltpu.HBM) for x in (states, w_key, w_value)))


def causal_bias(count):
    key_pos = lax.broadcasted_iota(jnp.int32, (count, count), 0)
    row_pos = lax.broadcasted_iota(jnp.int32, (count, count), 1)
    return jnp.where(key_pos <= row_pos, 0.0, -jnp.inf).astype(F32)


def slot_bias(position, slots, count, dims):
    row = lax.broadcasted_iota(jnp.int32, dims, 0)
    bias = jnp.full(dims, -jnp.inf, F32)
    for at, slot in enumerate(slots):
        level = jnp.where((position ^ slot) < position, 0.0, -jnp.inf).astype(F32)
        bias = jnp.where((row >= at * count) & (row < (at + 1) * count), level, bias)
    return bias


def fill_padded(wide_ref, rows_ref):
    shown = rows_ref.shape[0]
    padded = wide_ref.shape[0]
    tail = shown // 8 * 8
    if padded > tail:
        wide_ref[tail:, :] = jnp.zeros((padded - tail, wide_ref.shape[1]), F32)
    wide_ref[:shown, :] = rows_ref[...].astype(F32)


def own_stats_kernel(q_ref, g_ref, k_ref, v_ref, stats_ref, bias_ref):
    bias_ref[...] = causal_bias(bias_ref.shape[0])
    for kv in range(k_ref.shape[1] // HD):
        keys = k_ref[:, lanes(kv)]
        values = v_ref[:, lanes(kv)]
        for head in range(kv * GROUP, (kv + 1) * GROUP):
            scores = dot(keys, q_ref[:, lanes(head)], LAST) * SCALE2 + bias_ref[...]
            top = jnp.max(scores, axis=0, keepdims=True)
            weights = jnp.exp2(scores - top)
            dprobs = dot(values, g_ref[:, lanes(head)], LAST)
            stats_ref[head, 0:1, :] = top
            stats_ref[head, 1:2, :] = jnp.sum(weights, axis=0, keepdims=True)
            stats_ref[head, 2:3, :] = jnp.sum(weights * dprobs, axis=0, keepdims=True)


def own_stats(queries, out_grad, keys_own, values_own):
    rows = queries.shape[0]
    heads = queries.shape[1] // HD
    return pl.pallas_call(
        own_stats_kernel,
        name="own_stats",
        in_specs=[VMEM] * 4,
        out_specs=VMEM,
        out_shape=shape((heads, 8, rows), F32),
        scratch_shapes=[pltpu.VMEM((rows, rows), F32)],
        compiler_params=params(12),
        cost_estimate=cost(20 * heads * rows * rows * HD, 4 * rows * heads * HD),
    )(queries, out_grad, keys_own, values_own)


def even_stats_kernel(
    count, evens, odds, seg_ref, q_ref, g_ref, even_ref, own_ref,
    stats_ref, even_bias_ref, odd_bias_ref, wide_ref,
):
    position = seg_ref[0]
    width = even_ref.shape[1] // 2
    even_bias_ref[...] = slot_bias(position, evens, count, even_bias_ref.shape)
    odd_bias_ref[...] = slot_bias(position, odds, count, odd_bias_ref.shape)
    fill_padded(wide_ref, even_ref)
    for kv in range(width // HD):
        keys = wide_ref[:, lanes(kv)].astype(BF16)
        values = wide_ref[:, lanes(width // HD + kv)].astype(BF16)
        for head in range(kv * GROUP, (kv + 1) * GROUP):
            scores = dot(keys, q_ref[:, lanes(head)], LAST) * SCALE2 + even_bias_ref[...]
            own_top = own_ref[head, 0:1, :]
            top = jnp.maximum(jnp.max(scores, axis=0, keepdims=True), own_top)
            weights = jnp.exp2(scores - top)
            shrink = jnp.exp2(own_top - top)
            dprobs = dot(values, g_ref[:, lanes(head)], LAST)
            total = jnp.sum(weights, axis=0, keepdims=True)
            mixed = jnp.sum(weights * dprobs, axis=0, keepdims=True)
            stats_ref[head, 0:1, :] = top
            stats_ref[head, 1:2, :] = total + own_ref[head, 1:2, :] * shrink
            stats_ref[head, 2:3, :] = mixed + own_ref[head, 2:3, :] * shrink


def even_stats(position, queries, out_grad, even, own, count, evens, odds):
    rows = queries.shape[0]
    heads = queries.shape[1] // HD
    padded = round_up(even.shape[0], 16)
    return pl.pallas_call(
        functools.partial(even_stats_kernel, count, evens, odds),
        name="even_stats",
        in_specs=[SMEM] + [VMEM] * 4,
        out_specs=[VMEM] * 3,
        out_shape=[
            shape((heads, 8, rows), F32),
            shape((padded, rows), F32),
            shape((round_up(len(odds) * count, 16), rows), F32),
        ],
        scratch_shapes=[pltpu.VMEM((padded, even.shape[1]), F32)],
        compiler_params=params(12 if padded <= 512 else 32),
        cost_estimate=cost(20 * heads * rows * padded * HD, 4 * rows * heads * HD),
    )(position, queries, out_grad, even, own)


def slots_kernel(
    last, q_ref, g_ref, slots_ref, before_ref, bias_ref,
    ds_ref, stats_ref, keys_ref, grad_ref, wide_ref,
):
    shown = grad_ref.shape[0]
    kv_local = keys_ref.shape[1] // HD
    width = kv_local * HD
    if last:
        keys_ref[...] = slots_ref[:, :width]
    else:
        fill_padded(wide_ref, slots_ref)
        keys_ref[...] = wide_ref[:, :width].astype(BF16)
    for kv in range(kv_local):
        keys = (slots_ref if last else keys_ref)[:, lanes(kv)]
        values = (slots_ref if last else wide_ref)[:, lanes(kv_local + kv)].astype(BF16)
        heads = range(kv * GROUP, (kv + 1) * GROUP)
        all_dscores, all_probs = [], []
        for head in heads:
            scores = dot(keys, q_ref[:, lanes(head)], LAST) * SCALE2 + bias_ref[...]
            dprobs = dot(values, g_ref[:, lanes(head)], LAST)
            old_top = before_ref[head, 0:1, :]
            if last:
                top = jnp.maximum(jnp.max(scores, axis=0, keepdims=True), old_top)
                weights = jnp.exp2(scores - top)
                shrink = jnp.exp2(old_top - top)
                total = jnp.sum(weights, axis=0, keepdims=True)
                inverse = 1.0 / (total + before_ref[head, 1:2, :] * shrink)
                mixed = jnp.sum(weights * dprobs, axis=0, keepdims=True)
                delta = (mixed + before_ref[head, 2:3, :] * shrink) * inverse
                probs = weights * inverse
                stats_ref[head, 0:1, :] = top
                stats_ref[head, 1:2, :] = inverse
                stats_ref[head, 2:3, :] = delta
            else:
                probs = jnp.exp2(scores - old_top) * before_ref[head, 1:2, :]
                delta = before_ref[head, 2:3, :]
            dscores = (probs * (dprobs - delta)).astype(BF16)
            ds_ref[head] = dscores
            all_dscores.append(dscores)
            all_probs.append(probs.astype(BF16))
        queries = jnp.concatenate([q_ref[:, lanes(head)] for head in heads], 0)
        grads = jnp.concatenate([g_ref[:, lanes(head)] for head in heads], 0)
        key_part = dot(jnp.concatenate(all_dscores, 1), queries) * SCALE
        value_part = dot(jnp.concatenate(all_probs, 1), grads)
        grad_ref[:, lanes(kv)] = key_part[:shown].astype(grad_ref.dtype)
        grad_ref[:, lanes(kv_local + kv)] = value_part[:shown].astype(grad_ref.dtype)
    if not last:
        stats_ref[...] = jnp.zeros_like(stats_ref)


def slots_part(last, shown, queries, out_grad, slots, before, bias):
    rows = queries.shape[0]
    width = slots.shape[1] // 2
    heads = queries.shape[1] // HD
    padded = round_up(shown, 16)
    return pl.pallas_call(
        functools.partial(slots_kernel, last),
        name="odd_slots" if last else "even_slots",
        in_specs=[VMEM] * 5,
        out_specs=[VMEM] * 4,
        out_shape=[
            shape((heads, padded, rows)),
            shape((heads, 8, rows) if last else (8, HD), F32),
            shape((padded, width)),
            shape((shown, 2 * width), BF16 if last else F32),
        ],
        scratch_shapes=[pltpu.VMEM((padded, 2 * width), F32)],
        compiler_params=params(16 if padded <= 512 else 40),
        cost_estimate=cost(30 * heads * rows * padded * HD, 4 * rows * heads * HD),
    )(queries, out_grad, slots, before, bias)


def own_grads_kernel(
    heads, carried, q_ref, g_ref, k_ref, v_ref, ok_ref, ek_ref, ods_ref, eds_ref, stats_ref, *rest
):
    *sums, dq_out, dk_out, dv_out, dk_next, dv_next, bias_ref, dq_ref, grad_ref, sems = rest
    bias_ref[...] = causal_bias(bias_ref.shape[0])
    copies = []

    def send(source, target, at):
        copies.append(pltpu.make_async_copy(source, target, sems.at[at]))
        copies[-1].start()

    for kv in range(heads[0] // GROUP, heads[-1] // GROUP + 1):
        keys = k_ref[:, lanes(kv)]
        values = v_ref[:, lanes(kv)]
        keys_t = jnp.concatenate([ok_ref[:, lanes(kv)], ek_ref[:, lanes(kv)], keys], 0).T
        mine = [head for head in heads if head // GROUP == kv]
        all_dscores, all_probs = [], []
        for head in mine:
            scores = dot(keys, q_ref[:, lanes(head)], LAST) * SCALE2 + bias_ref[...]
            probs = jnp.exp2(scores - stats_ref[head, 0:1, :]) * stats_ref[head, 1:2, :]
            dprobs = dot(values, g_ref[:, lanes(head)], LAST)
            dscores = (probs * (dprobs - stats_ref[head, 2:3, :])).astype(BF16)
            all_dscores.append(dscores)
            all_probs.append(probs.astype(BF16))
            dquery = dot(keys_t, jnp.concatenate([ods_ref[head], eds_ref[head], dscores], 0))
            dq_ref[:, lanes(head - heads[0])] = (dquery * SCALE).T.astype(BF16)
        if mine[-1] == heads[-1]:
            send(dq_ref, dq_out.at[:, pl.ds(heads[0] * HD, len(heads) * HD)], 0)
        queries = jnp.concatenate([q_ref[:, lanes(head)] for head in mine], 0)
        grads = jnp.concatenate([g_ref[:, lanes(head)] for head in mine], 0)
        key_part = dot(jnp.concatenate(all_dscores, 1), queries)
        value_part = dot(jnp.concatenate(all_probs, 1), grads)
        if carried and mine[0] == heads[0]:
            key_part = key_part + sums[-2][...]
            value_part = value_part + sums[-1][...]
        if mine[-1] % GROUP == GROUP - 1:
            grad_ref[:, lanes(2 * kv)] = (key_part * SCALE).astype(BF16)
            grad_ref[:, lanes(2 * kv + 1)] = value_part.astype(BF16)
            column = pl.ds(kv * HD, HD)
            send(grad_ref.at[:, pl.ds(2 * kv * HD, HD)], dk_out.at[:, column], 2 * kv + 1)
            send(grad_ref.at[:, pl.ds((2 * kv + 1) * HD, HD)], dv_out.at[:, column], 2 * kv + 2)
        else:
            dk_next[...] = key_part
            dv_next[...] = value_part
    if heads[-1] % GROUP == GROUP - 1:
        dk_next[...] = jnp.zeros_like(dk_next)
        dv_next[...] = jnp.zeros_like(dv_next)
    for copy in copies:
        copy.wait()


def own_grads(heads, operands, earlier):
    queries, keys, odd_keys, even_keys = operands[0], operands[2], operands[4], operands[5]
    rows = queries.shape[0]
    kv_local = keys.shape[1] // HD
    padded = odd_keys.shape[0] + even_keys.shape[0]
    return pl.pallas_call(
        functools.partial(own_grads_kernel, heads, heads[0] % GROUP != 0),
        name="own_grads",
        in_specs=[VMEM] * len(operands) + [HBM, HBM, HBM, VMEM, VMEM][: len(earlier)],
        out_specs=[HBM, HBM, HBM, VMEM, VMEM],
        out_shape=[shape(queries.shape), shape(keys.shape), shape(keys.shape)]
        + [shape((rows, HD), F32)] * 2,
        input_output_aliases={len(operands) + at: at for at in range(3)} if earlier else {},
        scratch_shapes=[
            pltpu.VMEM((rows, rows), F32),
            pltpu.VMEM((rows, len(heads) * HD), BF16),
            pltpu.VMEM((rows, 2 * kv_local * HD), BF16),
            pltpu.SemaphoreType.DMA((2 * kv_local + 1,)),
        ],
        compiler_params=params(16 if padded <= 512 else 32),
        cost_estimate=cost(20 * len(heads) * rows * rows * HD, 4 * rows * len(heads) * HD),
    )(*operands, *earlier)


def state_kernel(chunk, blocks, mine_ref, emitted_ref, wk_ref, wv_ref, *out_refs):
    width = wk_ref.shape[1]
    keys = emitted_ref[:, :width]
    values = emitted_ref[:, width:]
    for (key, split, part), out_ref in zip(blocks, out_refs):
        wide = out_ref.shape[1]
        first = (mine_ref[0] ^ key) * split + part
        for step in range(wide // chunk):
            rows = pl.ds(pl.multiple_of(first * wide + step * chunk, chunk), chunk)
            total = dot(keys, wk_ref[rows, :], LAST) + dot(values, wv_ref[rows, :], LAST)
            out_ref[:, step * chunk : (step + 1) * chunk] = total.astype(BF16)


def state_part(mine, emitted, w_key, w_value, wide, blocks, chunk=512):
    rows = emitted.shape[0]
    width = w_key.shape[1]
    columns = sum(wide // split for _, split, _ in blocks)
    return pl.pallas_call(
        functools.partial(state_kernel, chunk, blocks),
        name="state_part",
        in_specs=[SMEM] + [VMEM] * 3,
        out_specs=[VMEM] * len(blocks),
        out_shape=[shape((rows, wide // split)) for _, split, _ in blocks],
        compiler_params=params(14),
        cost_estimate=cost(4 * rows * columns * width, 4 * columns * width),
    )(mine, emitted, w_key, w_value)


def exchange(block, axis, size, key):
    return lax.ppermute(block, axis, [(i, i ^ key) for i in range(size)])


def per_device(
    queries, keys_own, values_own, out_grad, summary_states, w_key, w_value, summary_grad
):
    kv_local = keys_own.shape[1] // HD
    count = summary_states.shape[0]
    n_seg = lax.axis_size("seg")
    n_tp = lax.axis_size("tp")
    position = lax.axis_index("seg").astype(jnp.int32).reshape(1)
    mine = lax.axis_index("tp").astype(jnp.int32).reshape(1)

    projected = project(summary_states, w_key, w_value)
    own = own_stats(queries, out_grad, keys_own, values_own)

    middle = [j for j in range(4, n_seg, 4)]
    last = [j for j in range(2, n_seg, 4)]
    near, far = [0], middle + last
    evens = (near + far)[1:]
    odds = [j + 1 for j in near + far]
    chunks = {j: exchange(projected, "seg", n_seg, j) for j in range(2, n_seg, 2)}
    chunks[0] = projected
    shown = len(odds) * count
    padding = round_up(shown, 16) - shown
    odd = jnp.concatenate(
        [
            exchange(jnp.concatenate([chunks[j] for j in group], 0), "seg", n_seg, 1)
            for group in (near, middle, last)
        ]
        + [jnp.zeros((padding, projected.shape[1]), BF16)] * (padding > 0),
        0,
    )
    even = jnp.concatenate([chunks[j] for j in evens], 0)

    before, even_bias, odd_bias = even_stats(
        position, queries, out_grad, even, own, count, evens, odds
    )
    odd_ds, stats, odd_keys, odd_grad = slots_part(
        True, shown, queries, out_grad, odd, before, odd_bias
    )

    got = exchange(odd_grad, "seg", n_seg, 1)
    even_ds, _, even_keys, even_grad = slots_part(
        False, even.shape[0], queries, out_grad, even, stats, even_bias
    )
    operands = [
        queries, out_grad, keys_own, values_own, odd_keys, even_keys, odd_ds, even_ds, stats
    ]
    cuts = [0, kv_local * GROUP * 4 // 16, kv_local * GROUP * 8 // 16, kv_local * GROUP]
    shares = [range(*pair) for pair in zip(cuts, cuts[1:])]
    begun = own_grads(shares[0], operands, [])
    got, even_grad, begun = lax.optimization_barrier((got, even_grad, begun))
    blocks = {}
    for j in sorted(evens, key=lambda j: (j.bit_count(), -j)):
        at = evens.index(j) * count
        block = got[at + count : at + 2 * count].astype(F32) + even_grad[at : at + count]
        block = block.astype(BF16)
        blocks[j] = exchange(block, "seg", n_seg, j)
    begun = own_grads(shares[1], operands, begun)
    blocks, begun = lax.optimization_barrier((blocks, begun))
    emitted = got[:count].astype(F32)
    for block in blocks.values():
        emitted = emitted + block.astype(F32)
    emitted = emitted.astype(BF16)

    wide = w_key.shape[0] // n_tp
    halves = 1
    far = range(n_tp - 1, 1, -1)
    calls = [[(j, halves, part) for j in far if j & 1] for part in range(halves)]
    calls.append([(j, halves, part) for part in range(halves) for j in far if not j & 1])
    terms = {}
    for blocks in calls:
        results = state_part(mine, emitted, w_key, w_value, wide, blocks)
        terms.update(((j, part), result) for (j, _, part), result in zip(blocks, results))
    for part in range(halves):
        bit = 1
        while bit < n_tp:
            for j in [j for j in far if (j, part) in terms and j & bit and j > bit]:
                got = exchange(terms.pop((j, part)).astype(BF16), "tp", n_tp, bit)
                total = terms[j ^ bit, part].astype(F32) + got.astype(F32)
                terms[j ^ bit, part] = total.astype(BF16)
            bit *= 2
    late = {at: terms[at] for at in terms if at[1] == halves - 1}
    late, emitted, begun = lax.optimization_barrier((late, emitted, begun))
    terms.update(late)
    arrived = {at: exchange(terms[at], "tp", n_tp, at[0]) for at in sorted(terms, key=lambda at: at[1])}
    other, state = state_part(mine, emitted, w_key, w_value, wide, [(1, 1, 0), (0, 1, 0)])
    state = state.astype(F32) + exchange(other, "tp", n_tp, 1).astype(F32)
    for j in sorted({j for j, _ in arrived}):
        pieces = [arrived[j, part] for part in range(halves)]
        state = state + jnp.concatenate(pieces, 1).astype(F32)
    state_grad = (state + summary_grad.astype(F32)).astype(BF16)

    query_grad, key_grad, value_grad, *_ = own_grads(shares[2], operands, begun)
    return (query_grad, key_grad, value_grad, state_grad)


def solution(mesh):
    placed = (
        P("seg", "tp"),
        P("seg", "tp"),
        P("seg", "tp"),
        P("seg", "tp"),
        P("seg", None),
        P(None, "tp"),
        P(None, "tp"),
        P("seg", "tp"),
    )
    return jax.shard_map(
        per_device,
        mesh=mesh,
        in_specs=placed,
        out_specs=(P("seg", "tp"), P("seg", "tp"), P("seg", "tp"), P("seg", "tp")),
        check_vma=False,
    )
```
